32 devices in a mesh: row: 4 (over y, x), col: 8 (over z, core).
Axes of the slice: x: 2, y: 2, z: 4, core: 2. Of those that a mesh axis runs over, the one named last changes fastest.
Arguments:
- features: bfloat16 [4096, 256], P(('row', 'col')), may hold values from -6 to 6
- weight: bfloat16 [256, 256], replicated, may hold values from -0.375 to 0.375
- tiles: bfloat16 [384, 128, 128], P(('row', 'col')), may hold values from 0 to 0.0099487305
- tile_pos: int32 [384], P(('row', 'col')), may hold values from -1 to 31, as said below
- edge_keep: int32 [2, 384], P(None, ('row', 'col')), may hold values 0 or 1
- feature_keep: int32 [2, 256], replicated, may hold values 0 or 1
- negatives: int32 [4096, 1024], P(('row', 'col')), may hold values from 0 to 511, as said below
Outputs:
- node_loss: float32 [4096], P(('row', 'col'))
- weight_grad: float32 [256, 256], replicated
The draws below stay inside these ranges and needn't reach their ends.
Inputs may be any that keep to these rules, and one draw needn't show every extreme that they name: `tile_pos`: on each device the first count slots hold distinct positions and the rest are -1; every device has at least one tile, at least one device has all 12 slots filled. `negatives`: indices into the node's column group, each node's list in ascending order; an index may repeat within a node's list.
All inputs are finite; a program needn't handle non-finite values. No bound on the sum of `edge_keep` on one device may be relied on, other than what follows from the above.
Results may differ from the reference program's by a relative error of at most 0.0035.
Values may be sent and summed in bfloat16 or wider, within the bound.
A program may use at most 64 MiB of HBM per device.

```python
import jax
import jax.numpy as jnp
from jax import lax

FEAT = 256
NODE_DEV = 128
NEG = 1024
TR = 4
TC = 8
KT = 12
GROUP = 512
NODES = 4096
N_ROW = 4
N_COL = 8


def draw_tile_pos(key, part):
    key = jax.random.fold_in(key, 11)
    devcount = N_ROW * N_COL
    first, second, third, fourth = jax.random.split(key, 4)
    upper = jax.random.randint(first, (devcount,), 1, KT + 1)
    lower = jax.random.randint(second, (devcount,), 1, KT + 1)
    filled = jnp.maximum(1, upper * lower // KT)
    busiest = jax.random.randint(third, (), 0, devcount)
    filled = jnp.where(jnp.arange(devcount) == busiest, KT, filled)
    orders = jax.vmap(lambda k: jax.random.permutation(k, TR * TC))(jax.random.split(fourth, devcount))[:, :KT]
    slots = jnp.arange(KT)
    chosen = jnp.where(slots[None, :] < filled[:, None], orders, -1)
    return chosen.reshape(-1).astype(jnp.int32)


def draw_negatives(key, part):
    key = jax.random.fold_in(key, 23)
    span = min(16, NODE_DEV)
    hot_count = NEG * 3 // 4
    cold_count = NEG - hot_count
    first, second, third, fourth, fifth = jax.random.split(key, 5)
    node = jnp.arange(NODES)
    own_block = node // NODE_DEV // N_COL
    side = jax.random.randint(first, (NODES,), 0, 2)
    other = (own_block + jax.random.randint(second, (NODES,), 1, max(N_ROW, 2))) % N_ROW
    block = jnp.where(side == 1, own_block, other)
    start = block * NODE_DEV + jax.random.randint(third, (NODES,), 0, NODE_DEV - span + 1)
    hot = start[:, None] + jax.random.randint(fourth, (NODES, hot_count), 0, span)
    cold = jax.random.randint(fifth, (NODES, cold_count), 0, GROUP)
    merged = jnp.concatenate([hot, cold], axis=1)
    return jnp.sort(merged, axis=1).astype(jnp.int32)


def touch_ends(array, stream_key, low, high):
    shape = array.shape
    index_at = [jax.random.randint(jax.random.fold_in(stream_key, axis), (), 0, shape[axis]) for axis in range(len(shape))]
    array = array.at[tuple(index_at)].set(low)
    longest = shape.index(max(shape))
    index_at[longest] = (index_at[longest] + 1) % shape[longest]
    return array.at[tuple(index_at)].set(high)


def levels(own_key, extent, cuts, least, largest):
    def one(axis_at, parts):
        heights = jax.random.uniform(jax.random.fold_in(jax.random.fold_in(own_key, 6), axis_at), (parts,), jnp.float32, least / len(cuts), largest / len(cuts))
        return jnp.repeat(jnp.exp(heights), extent[axis_at] // parts).reshape((-1,) + (1,) * (len(extent) - axis_at - 1))

    factor_of = one(*cuts[0])
    for cut in cuts[1:]:
        factor_of = factor_of * one(*cut)
    return factor_of


def gaussian(stream_key, dims, deviation, most, shards=(), held_as=jnp.bfloat16):
    factor_of = levels(stream_key, dims, shards, -0.22, 0.18) if shards else 1.0
    result = jax.random.normal(stream_key, dims, jnp.float32) * deviation * factor_of
    return jnp.minimum(jnp.maximum(result, -most), most).astype(held_as)


def setup_inputs(seed: int = 0) -> dict:
    streams_of = jax.random.split(jax.random.key(seed), 8)
    return {
        "features": gaussian(streams_of[0], (NODES, FEAT), 1.0, 6.0, ((0, 32),)),
        "weight": gaussian(streams_of[1], (FEAT, FEAT), FEAT ** -0.5, 0.375),
        "tiles": jnp.clip(0.0099487305 * jax.random.uniform(streams_of[2], (N_ROW * N_COL * KT, 128, 128), jnp.float32) ** levels(streams_of[2], (N_ROW * N_COL * KT, 128, 128), ((0, 32),), -0.2, 0.2), 0.0, 0.0099487305).astype(jnp.bfloat16),
        "tile_pos": draw_tile_pos(jax.random.fold_in(streams_of[7], 71), 0),
        "edge_keep": touch_ends((jax.random.randint(streams_of[4], (2, N_ROW * N_COL * KT), 0, 10) < 7).astype(jnp.int32), jax.random.fold_in(streams_of[4], 1), 0, 1),
        "feature_keep": touch_ends((jax.random.randint(streams_of[5], (2, FEAT), 0, 10) < 7).astype(jnp.int32), jax.random.fold_in(streams_of[5], 1), 0, 1),
        "negatives": draw_negatives(jax.random.fold_in(streams_of[7], 71), 0),
    }


tau = 0.5
eps = 1e-06

def reference(features, weight, tiles, tile_pos, edge_keep, feature_keep, negatives):
    xrows = features.reshape(N_ROW, TC, 128, FEAT)
    tiles_grid = tiles.reshape(N_ROW, N_COL, KT, 128, 128)
    pos_grid = tile_pos.reshape(N_ROW, N_COL, KT)
    keep_grid = edge_keep.astype(jnp.float32).reshape(2, N_ROW, N_COL, KT)
    fkeep = feature_keep.astype(jnp.float32)

    def group_agg(colidx):

        def add_device(total, rowidx):
            xr = xrows[rowidx]
            pos = pos_grid[rowidx, colidx]
            valid = (pos >= 0).astype(jnp.float32)
            clamped = jnp.maximum(pos, 0)
            trow = clamped // TC
            tcol = clamped % TC
            xt = xr[tcol].astype(jnp.float32)
            prod = jnp.einsum('kab,kbf->kaf', tiles_grid[rowidx, colidx].astype(jnp.float32), xt, precision=lax.Precision.HIGHEST)
            wts = keep_grid[:, rowidx, colidx] * valid[None, :]
            onehot = (trow[None, :] == jnp.arange(TR)[:, None]).astype(jnp.float32)
            term = jnp.einsum('vk,tk,kaf->vtaf', wts, onehot, prod, precision=lax.Precision.HIGHEST)
            rounded = lax.optimization_barrier(term.astype(jnp.bfloat16)).astype(jnp.float32)
            return (total + rounded, None)
        total = lax.scan(add_device, jnp.zeros((2, TR, 128, FEAT), jnp.float32), jnp.arange(N_ROW))[0]
        return total.reshape(2, GROUP, FEAT) * fkeep[:, None, :]
    agg = lax.map(group_agg, jnp.arange(N_COL))
    agg_b = agg.astype(jnp.bfloat16)
    neg_groups = negatives.reshape(N_ROW, N_COL, NODE_DEV, NEG).transpose(1, 0, 2, 3).reshape(N_COL, GROUP, NEG)
    coef = 1.0 / (2.0 * tau * jnp.sqrt(jnp.float32(NODES)))

    def group_loss(items):
        pb, negs = items
        z = jnp.einsum('vnf,fg->vng', pb.astype(jnp.float32), weight.astype(jnp.float32), precision=lax.Precision.HIGHEST)
        rinv = lax.rsqrt(lax.optimization_barrier(jnp.sum(z * z, -1, keepdims=True)) + eps)
        emb = z * rinv
        emb_b = emb.astype(jnp.bfloat16)
        hb1, hb2 = (emb_b[0], emb_b[1])
        h1f, h2f = (hb1.astype(jnp.float32), hb2.astype(jnp.float32))
        counts = jnp.zeros((GROUP, GROUP), jnp.float32).at[jnp.arange(GROUP)[:, None], negs].add(1.0)
        pos = lax.optimization_barrier(jnp.sum(h1f * h2f, -1)) / tau
        s12 = jnp.dot(hb1, hb2.T, preferred_element_type=jnp.float32) / tau
        s21 = jnp.dot(hb2, hb1.T, preferred_element_type=jnp.float32) / tau
        e12 = counts * jnp.exp(s12)
        e21 = counts * jnp.exp(s21)
        tot1 = jnp.exp(pos) + lax.optimization_barrier(jnp.sum(e12, 1))
        tot2 = jnp.exp(pos) + lax.optimization_barrier(jnp.sum(e21, 1))
        loss = 0.5 * (jnp.log(tot1) - pos + (jnp.log(tot2) - pos))
        p1 = jnp.exp(pos) / tot1
        p2 = jnp.exp(pos) / tot2
        q1 = (e12 / tot1[:, None]).astype(jnp.bfloat16)
        q2 = (e21 / tot2[:, None]).astype(jnp.bfloat16)
        both = (p1 + p2 - 2.0)[:, None]
        d1 = coef * (both * h2f + jnp.dot(q1, hb2, preferred_element_type=jnp.float32) + jnp.dot(q2.T, hb2, preferred_element_type=jnp.float32))
        d2 = coef * (both * h1f + jnp.dot(q2, hb1, preferred_element_type=jnp.float32) + jnp.dot(q1.T, hb1, preferred_element_type=jnp.float32))
        dh = jnp.stack([d1, d2])
        dz = (dh - emb * lax.optimization_barrier(jnp.sum(emb * dh, -1, keepdims=True))) * rinv
        grad = jnp.einsum('vnf,vng->fg', pb.astype(jnp.float32), dz, precision=lax.Precision.HIGHEST)
        return (loss, grad)
    losses, grads = lax.map(group_loss, (agg_b, neg_groups))
    node_loss = losses.reshape(N_COL, N_ROW, NODE_DEV).transpose(1, 0, 2).reshape(NODES)
    return (node_loss, lax.optimization_barrier(jnp.sum(grads, 0)))
```

```python
import functools

import jax
import jax.numpy as jnp
from jax import lax
from jax.experimental import pallas as pl
from jax.experimental.pallas import tpu as pltpu
from jax.sharding import PartitionSpec as P

tau = 0.5
eps = 1e-06
F32 = jnp.float32
BF16 = jnp.bfloat16
MESH = pl.DeviceIdType.MESH


def loop(start, stop, body):
    if stop - start <= 8:
        for i in range(start, stop):
            body(i)
    else:
        def step(i, carry):
            body(i)
            return carry
        lax.fori_loop(start, stop, step, 0)


def count_kernel(neg_ref, cnt_ref):
    rows, n_neg = neg_ref.shape
    blocks = cnt_ref.shape[1] // 128
    chunks = n_neg // 128
    per = 4 if blocks % 4 == 0 else 1
    lane = lax.broadcasted_iota(jnp.int32, (8, 128), 1)

    def rank(parts, target):
        total = jnp.zeros((8, 128), jnp.int32)
        for part in parts:
            low = jnp.zeros((8, 128), jnp.int32)
            for step in (64, 32, 16, 8, 4, 2, 1):
                seen = jnp.take_along_axis(part, low + (step - 1), axis=1, mode="promise_in_bounds")
                low = jnp.where(seen <= target, low + step, low)
            seen = jnp.take_along_axis(part, low, axis=1, mode="promise_in_bounds")
            total = total + jnp.where(seen <= target, low + 1, low)
        return total

    def row_step(i, carry):
        base = pl.multiple_of(i * 8, 8)
        parts = [neg_ref[pl.ds(base, 8), k * 128 : (k + 1) * 128] for k in range(chunks)]

        def block_step(g, before):
            for j in range(per):
                at = pl.multiple_of((g * per + j) * 128, 128)
                now = rank(parts, lane + at)
                rolled = pltpu.roll(now, 1, 1)
                shifted = jnp.where(lane == 0, before, rolled)
                cnt_ref[pl.ds(base, 8), pl.ds(at, 128)] = (now - shifted).astype(F32)
                before = rolled
            return before

        first = jnp.zeros((8, 128), jnp.int32)
        if blocks == per:
            block_step(0, first)
        else:
            lax.fori_loop(0, blocks // per, block_step, first)
        return carry

    lax.fori_loop(0, rows // 8, row_step, 0)


def step_kernel(
    R, C,
    feat, weight, tiles, pos_ref, keep_ref, fkeep, cnt,
    loss_out, grad_out,
    xg, xcat, pbuf, rbuf, gbuf, embf, embb, rinv, eb, wacc, wbuf, wr, ws, wc, wd, obuf,
    f_send, f_recv, s_send, s_recv, p_send, p_recv, g_send, g_recv,
    a_send, a_recv, b_send, b_recv, c_send, c_recv, d_send, d_recv,
):
    nodes, width = feat.shape
    slots = tiles.shape[0]
    chips = C // 2
    cr = wr.shape[1]
    cc = wc.shape[1]
    me_r = lax.axis_index("row")
    me_c = lax.axis_index("col")
    chip = me_c // 2
    core = me_c % 2
    sib = chip * 2 + (1 - core)

    def at_row(o):
        return lax.rem(me_r + o, R)

    def from_row(o):
        return lax.rem(me_r + R - o, R)

    def at_col(o):
        return lax.rem(me_c + o, C)

    def from_col(o):
        return lax.rem(me_c + C - o, C)

    def copy(src, dst, send, recv, r, c):
        return pltpu.make_async_remote_copy(
            src_ref=src, dst_ref=dst, send_sem=send, recv_sem=recv,
            device_id=(r, c), device_id_type=MESH,
        )

    barrier = pltpu.get_barrier_semaphore()
    loop(1, R, lambda o: pl.semaphore_signal(barrier, inc=1, device_id=(at_row(o), me_c), device_id_type=MESH))
    loop(1, C, lambda o: pl.semaphore_signal(barrier, inc=1, device_id=(me_r, at_col(o)), device_id_type=MESH))
    pl.semaphore_wait(barrier, R + C - 2)

    def far(o):
        to = lax.rem(chip + o, chips) * 2 + core
        return copy(feat, xg.at[me_c], f_send.at[o], f_recv.at[o], me_r, to)

    def near(o):
        if isinstance(o, int) and o == 0:
            return copy(feat, xg.at[me_c], s_send.at[0], s_recv.at[0], me_r, sib)
        slot = lax.rem(chip + chips - o, chips) * 2 + core
        return copy(xg.at[slot], xg.at[slot], s_send.at[o], s_recv.at[o], me_r, sib)

    loop(1, chips, lambda o: far(o).start())
    near(0).start()
    xg[me_c] = feat[...]

    def pass_on(o):
        far(o).wait_recv()
        near(o).start()

    loop(1, chips, pass_on)
    near(0).wait_recv()
    loop(1, chips, lambda o: near(o).wait_recv())

    where = [jnp.maximum(pos_ref[k], 0) for k in range(slots)]
    trow = [w // C for w in where]
    live = [[keep_ref[v, k] * (pos_ref[k] >= 0).astype(jnp.int32) for k in range(slots)] for v in range(2)]
    for k in range(slots):
        xcat[k * 128 : (k + 1) * 128, :] = xg[lax.rem(where[k], C)]

    def part_copy(o):
        return copy(pbuf.at[o], rbuf.at[o], p_send.at[o], p_recv.at[o], at_row(o), me_c)

    def part(o):
        t = at_row(o)
        out = []
        for v in range(2):
            lhs = []
            for k in range(slots):
                use = jnp.where(trow[k] == t, live[v][k], 0).astype(F32)
                lhs.append(tiles[k] * jnp.full((1, 128), use, F32).astype(BF16))
            out.append(jnp.dot(jnp.concatenate(lhs, axis=1), xcat[...], preferred_element_type=F32).astype(BF16))
        return out

    def part_send(o):
        first, second = part(o)
        pbuf[o, 0] = first
        pbuf[o, 1] = second
        part_copy(o).start()

    loop(1, R, part_send)
    mine = part(0)
    pbuf[0, 0] = mine[0]
    pbuf[0, 1] = mine[1]
    loop(1, R, lambda o: part_copy(o).wait_recv())

    for v in range(2):
        total = pbuf[0, v].astype(F32)
        if R <= 8:
            for o in range(1, R):
                total = total + rbuf[o, v].astype(F32)
        else:
            total = lax.fori_loop(1, R, lambda o, acc: acc + rbuf[o, v].astype(F32), total)
        total = total * fkeep[v : v + 1, :].astype(F32)
        gbuf[me_r, v] = total.astype(BF16)

    def agg_copy(o):
        return copy(gbuf.at[me_r], gbuf.at[me_r], g_send.at[o], g_recv.at[o], at_row(o), me_c)

    loop(1, R, lambda o: agg_copy(o).start())

    def embed(r):
        for v in range(2):
            z = jnp.dot(gbuf[r, v], weight[...], preferred_element_type=F32)
            scale = lax.rsqrt(jnp.sum(z * z, -1, keepdims=True) + eps)
            emb = z * scale
            rinv[r, v] = scale
            embf[r, v] = emb
            embb[r, v] = emb.astype(BF16)

    embed(me_r)
    h1 = embb[me_r, 0]
    h2 = embb[me_r, 1]
    h1f = h1.astype(F32)
    h2f = h2.astype(F32)
    pos = jnp.sum(h1f * h2f, -1, keepdims=True) / tau
    NT = (((1,), (1,)), ((), ()))
    TN = (((0,), (0,)), ((), ()))

    def scores(r):
        cols = pl.ds(pl.multiple_of(r * 128, 128), 128)
        counts = cnt[:, cols]
        s12 = lax.dot_general(h1, embb[r, 1], NT, preferred_element_type=F32) / tau
        s21 = lax.dot_general(h2, embb[r, 0], NT, preferred_element_type=F32) / tau
        eb[r, 0] = counts * jnp.exp(s12)
        eb[r, 1] = counts * jnp.exp(s21)

    scores(me_r)

    def arrived(o):
        r = from_row(o)
        agg_copy(o).wait_recv()
        embed(r)
        scores(r)

    loop(1, R, arrived)

    def row_sum(v):
        if R <= 8:
            total = eb[0, v]
            for r in range(1, R):
                total = total + eb[r, v]
        else:
            total = lax.fori_loop(1, R, lambda r, acc: acc + eb[r, v], eb[0, v])
        return jnp.sum(total, 1, keepdims=True)

    epos = jnp.exp(pos)
    tot1 = epos + row_sum(0)
    tot2 = epos + row_sum(1)
    loss = 0.5 * (jnp.log(tot1) - pos + (jnp.log(tot2) - pos))
    loss_out[...] = jnp.broadcast_to(loss, (nodes, 128)).T[0:1, :]
    both = epos / tot1 + epos / tot2 - 2.0
    coef = 1.0 / (2.0 * tau * float(R * C * nodes) ** 0.5)

    def dz_term(r, d_one, d_two):
        parts = []
        for v, d in enumerate((d_one, d_two)):
            emb = embf[r, v]
            dz = (d - emb * jnp.sum(emb * d, -1, keepdims=True)) * rinv[r, v]
            high = dz.astype(BF16)
            low = (dz - high.astype(F32)).astype(BF16)
            parts.append(jnp.concatenate([high, low], axis=1))
        rhs = jnp.concatenate(parts, axis=0)
        lhs = jnp.concatenate([gbuf[r, 0], gbuf[r, 1]], axis=0)
        return lax.dot_general(lhs, rhs, TN, preferred_element_type=F32)

    def weights(r):
        q1 = (eb[r, 0] / tot1).astype(BF16)
        q2 = (eb[r, 1] / tot2).astype(BF16)
        fore1 = jnp.dot(q1, embb[r, 1], preferred_element_type=F32)
        fore2 = jnp.dot(q2, embb[r, 0], preferred_element_type=F32)
        back1 = lax.dot_general(q2, h2, TN, preferred_element_type=F32)
        back2 = lax.dot_general(q1, h1, TN, preferred_element_type=F32)
        return fore1, fore2, back1, back2

    acc1, acc2, own1, own2 = weights(me_r)
    wacc[...] = jnp.zeros_like(wacc)

    def other(o, carry):
        r = from_row(o)
        fore1, fore2, back1, back2 = weights(r)
        wacc[...] += dz_term(r, coef * back1, coef * back2)
        return carry[0] + fore1, carry[1] + fore2

    if R <= 8:
        for o in range(1, R):
            acc1, acc2 = other(o, (acc1, acc2))
    else:
        acc1, acc2 = lax.fori_loop(1, R, other, (acc1, acc2))
    both_terms = wacc[...] + dz_term(
        me_r, coef * (both * h2f + acc1 + own1), coef * (both * h1f + acc2 + own2)
    )
    if wbuf.shape[0] > width:
        wbuf[...] = jnp.zeros_like(wbuf)
    wbuf[0:width, :] = both_terms[:, :width] + both_terms[:, width:]

    def a_copy(o):
        rows = pl.ds(pl.multiple_of(at_row(o) * cr, 8), cr)
        return copy(wbuf.at[rows, :], wr.at[o], a_send.at[o], a_recv.at[o], at_row(o), me_c)

    loop(1, R, lambda o: a_copy(o).start())
    own = wbuf[pl.ds(pl.multiple_of(me_r * cr, 8), cr), :]
    if ws.shape[0] > cr:
        ws[...] = jnp.zeros_like(ws)
    loop(1, R, lambda o: a_copy(o).wait_recv())
    if R <= 8:
        for o in range(1, R):
            own = own + wr[o]
    else:
        own = lax.fori_loop(1, R, lambda o, acc: acc + wr[o], own)
    ws[0:cr, :] = own

    def b_copy(o):
        rows = pl.ds(pl.multiple_of(at_col(o) * cc, 8), cc)
        return copy(ws.at[rows, :], wc.at[o], b_send.at[o], b_recv.at[o], me_r, at_col(o))

    loop(1, C, lambda o: b_copy(o).start())
    piece = ws[pl.ds(pl.multiple_of(me_c * cc, 8), cc), :]
    loop(1, C, lambda o: b_copy(o).wait_recv())
    if C <= 8:
        for o in range(1, C):
            piece = piece + wc[o]
    else:
        piece = lax.fori_loop(1, C, lambda o, acc: acc + wc[o], piece)
    mine_rows = pl.ds(pl.multiple_of(me_c * cc, 8), cc)
    wd[mine_rows, :] = piece

    def c_copy(o):
        return copy(wd.at[mine_rows, :], wd.at[mine_rows, :], c_send.at[o], c_recv.at[o], me_r, at_col(o))

    loop(1, C, lambda o: c_copy(o).start())
    loop(1, C, lambda o: c_copy(o).wait_recv())
    my_out = pl.ds(pl.multiple_of(me_r * cr, 8), cr)

    def d_copy(o):
        return copy(wd.at[pl.ds(0, cr), :], obuf.at[my_out, :], d_send.at[o], d_recv.at[o], at_row(o), me_c)

    loop(1, R, lambda o: d_copy(o).start())
    obuf[my_out, :] = wd[0:cr, :]
    loop(1, R, lambda o: d_copy(o).wait_recv())
    grad_out[...] = obuf[0:width, :]

    loop(1, chips, lambda o: far(o).wait_send())
    near(0).wait_send()
    loop(1, chips, lambda o: near(o).wait_send())
    loop(1, R, lambda o: part_copy(o).wait_send())
    loop(1, R, lambda o: agg_copy(o).wait_send())
    loop(1, R, lambda o: a_copy(o).wait_send())
    loop(1, C, lambda o: b_copy(o).wait_send())
    loop(1, C, lambda o: c_copy(o).wait_send())
    loop(1, R, lambda o: d_copy(o).wait_send())


def up(n, d, unit):
    return -(-(-(-n // d)) // unit) * unit


def shards(features, weight, tiles, tile_pos, edge_keep, feature_keep, negatives):
    nodes, width = features.shape
    slots = tiles.shape[0]
    R = lax.axis_size("row")
    C = lax.axis_size("col")
    group = R * nodes
    chips = C // 2
    counts = pl.pallas_call(
        count_kernel,
        out_shape=jax.ShapeDtypeStruct((nodes, group), F32),
        in_specs=[pl.BlockSpec(memory_space=pltpu.VMEM)],
        out_specs=pl.BlockSpec(memory_space=pltpu.VMEM),
        compiler_params=pltpu.CompilerParams(vmem_limit_bytes=16 << 20),
    )(negatives)
    cr = up(width, R, 8)
    cc = up(cr, C, 8)
    vmem = pl.BlockSpec(memory_space=pltpu.VMEM)
    smem = pl.BlockSpec(memory_space=pltpu.SMEM)
    sem = pltpu.SemaphoreType.DMA
    loss, grad = pl.pallas_call(
        functools.partial(step_kernel, R, C),
        out_shape=(
            jax.ShapeDtypeStruct((1, nodes), F32),
            jax.ShapeDtypeStruct((width, width), F32),
        ),
        in_specs=[vmem, vmem, vmem, smem, smem, vmem, vmem],
        out_specs=(vmem, vmem),
        scratch_shapes=[
            pltpu.VMEM((C, nodes, width), BF16),
            pltpu.VMEM((slots * 128, width), BF16),
            pltpu.VMEM((R, 2, nodes, width), BF16),
            pltpu.VMEM((R, 2, nodes, width), BF16),
            pltpu.VMEM((R, 2, nodes, width), BF16),
            pltpu.VMEM((R, 2, nodes, width), F32),
            pltpu.VMEM((R, 2, nodes, width), BF16),
            pltpu.VMEM((R, 2, nodes, 1), F32),
            pltpu.VMEM((R, 2, nodes, 128), F32),
            pltpu.VMEM((width, 2 * width), F32),
            pltpu.VMEM((R * cr, width), F32),
            pltpu.VMEM((R, cr, width), F32),
            pltpu.VMEM((C * cc, width), F32),
            pltpu.VMEM((C, cc, width), F32),
            pltpu.VMEM((C * cc, width), F32),
            pltpu.VMEM((R * cr, width), F32),
            sem((chips,)), sem((chips,)), sem((chips,)), sem((chips,)),
            sem((R,)), sem((R,)), sem((R,)), sem((R,)),
            sem((R,)), sem((R,)), sem((C,)), sem((C,)),
            sem((C,)), sem((C,)), sem((R,)), sem((R,)),
        ],
        compiler_params=pltpu.CompilerParams(
            collective_id=0, has_side_effects=True, vmem_limit_bytes=48 << 20
        ),
    )(features, weight, tiles, tile_pos, edge_keep, feature_keep, counts)
    return loss.reshape(nodes), grad


def solution(mesh):
    in_specs = (
        P(("row", "col"), None),
        P(),
        P(("row", "col"), None, None),
        P(("row", "col")),
        P(None, ("row", "col")),
        P(),
        P(("row", "col"), None),
    )
    out_specs = (P(("row", "col")), P())
    return jax.shard_map(shards, mesh=mesh, in_specs=in_specs, out_specs=out_specs, check_vma=False)
```

```python
import functools

import jax
import jax.numpy as jnp
from jax import lax
from jax.experimental import pallas as pl
from jax.experimental.pallas import tpu as pltpu
from jax.sharding import PartitionSpec as P

tau = 0.5
eps = 1e-06
F32 = jnp.float32
BF16 = jnp.bfloat16
MESH = pl.DeviceIdType.MESH


def loop(start, stop, body):
    if stop - start <= 8:
        for i in range(start, stop):
            body(i)
    else:
        def step(i, carry):
            body(i)
            return carry
        lax.fori_loop(start, stop, step, 0)


def spread_matrix(ref):
    n = ref.shape[0]
    stride = n // 128
    row = lax.broadcasted_iota(jnp.int32, (128, 128), 0)
    lane = lax.broadcasted_iota(jnp.int32, (128, 128), 1)
    for k in range(n // 128):
        here = lane == row // stride + k * (128 // stride)
        for s in range(stride):
            hit = jnp.logical_and(here, row % stride == s)
            ref[k * 128 : (k + 1) * 128, s * 128 : (s + 1) * 128] = jnp.where(hit, 1.0, 0.0).astype(BF16)


def spread(neg, matrix, out):
    low = (neg[...] & 255).astype(F32).astype(BF16)
    high = (neg[...] >> 8).astype(F32).astype(BF16)
    nodes = neg.shape[0]
    both = jnp.dot(jnp.concatenate([low, high], axis=0), matrix[...], preferred_element_type=F32)
    out[...] = (both[:nodes] + 256.0 * both[nodes:]).astype(jnp.int32)


def count_rows(i, tall, spread_ref, cnt):
    stride = spread_ref.shape[1] // 128
    blocks = cnt.shape[1] // 128
    per = 4 if blocks % 4 == 0 else 1
    rows = pl.ds(pl.multiple_of(i * tall, 8), tall)
    lane = lax.broadcasted_iota(jnp.int32, (tall, 128), 1)

    def take(part, index):
        return jnp.take_along_axis(part, index, axis=1, mode="promise_in_bounds")

    def block_step(g, before):
        starts = [pl.multiple_of((g * per + j) * 128, 128) for j in range(per)]
        targets = [lane + at for at in starts]
        last = spread_ref[rows, (stride - 1) * 128 : stride * 128]
        lows = [jnp.zeros((tall, 128), jnp.int32)] * per
        for step in (64, 32, 16, 8, 4, 2, 1):
            seen = [take(last, low + (step - 1)) for low in lows]
            lows = [jnp.where(x <= t, low + step, low) for x, t, low in zip(seen, targets, lows)]
        ranks = [low * stride for low in lows]
        for s in range(stride):
            part = spread_ref[rows, s * 128 : (s + 1) * 128]
            seen = [take(part, low) for low in lows]
            ranks = [jnp.where(x <= t, k + 1, k) for x, t, k in zip(seen, targets, ranks)]
        for at, now in zip(starts, ranks):
            rolled = pltpu.roll(now, 1, 1)
            cnt[rows, pl.ds(at, 128)] = (now - jnp.where(lane == 0, before, rolled)).astype(F32)
            before = rolled
        return before

    first = jnp.zeros((tall, 128), jnp.int32)
    if blocks == per:
        block_step(0, first)
    else:
        lax.fori_loop(0, blocks // per, block_step, first)


def step_kernel(
    R, C,
    feat, weight_in, tiles_in, pos_ref, keep_ref, fkeep, neg_in,
    loss_out, grad_out,
    weight, tiles, neg, matrix, spread_ref, cnt,
    xg, xcat, pbuf, rbuf, gbuf, embf, embb, rinv, eb, wacc, wbuf, wr, ws, wc, wd, obuf,
    f_send, f_recv, s_send, s_recv, p_send, p_recv, g_send, g_recv,
    a_send, a_recv, b_send, b_recv, c_send, c_recv, d_send, d_recv, l_sem,
):
    nodes, width = feat.shape
    slots = tiles.shape[0]
    chips = C // 2
    cr = wr.shape[1]
    cc = wc.shape[1]
    me_r = lax.axis_index("row")
    me_c = lax.axis_index("col")
    chip = me_c // 2
    core = me_c % 2
    sib = chip * 2 + (1 - core)

    def at_row(o):
        return lax.rem(me_r + o, R)

    def from_row(o):
        return lax.rem(me_r + R - o, R)

    def at_col(o):
        return lax.rem(me_c + o, C)

    def from_col(o):
        return lax.rem(me_c + C - o, C)

    def copy(src, dst, send, recv, r, c):
        return pltpu.make_async_remote_copy(
            src_ref=src, dst_ref=dst, send_sem=send, recv_sem=recv,
            device_id=(r, c), device_id_type=MESH,
        )

    loads = [
        pltpu.make_async_copy(neg_in, neg, l_sem.at[0]),
        pltpu.make_async_copy(tiles_in, tiles, l_sem.at[1]),
        pltpu.make_async_copy(weight_in, weight, l_sem.at[2]),
        pltpu.make_async_copy(feat, xg.at[me_c], l_sem.at[3]),
    ]
    for load in loads:
        load.start()

    barrier = pltpu.get_barrier_semaphore()
    loop(1, R, lambda o: pl.semaphore_signal(barrier, inc=1, device_id=(at_row(o), me_c), device_id_type=MESH))
    loop(1, C, lambda o: pl.semaphore_signal(barrier, inc=1, device_id=(me_r, at_col(o)), device_id_type=MESH))
    pl.semaphore_wait(barrier, R + C - 2)

    def far(o):
        to = lax.rem(chip + o, chips) * 2 + core
        return copy(feat, xg.at[me_c], f_send.at[o], f_recv.at[o], me_r, to)

    def near(o):
        if isinstance(o, int) and o == 0:
            return copy(feat, xg.at[me_c], s_send.at[0], s_recv.at[0], me_r, sib)
        slot = lax.rem(chip + chips - o, chips) * 2 + core
        return copy(xg.at[slot], xg.at[slot], s_send.at[o], s_recv.at[o], me_r, sib)

    loop(1, chips, lambda o: far(o).start())
    near(0).start()
    spread_matrix(matrix)
    loads[0].wait()
    spread(neg, matrix, spread_ref)
    tall = 32
    turns = nodes // tall

    def pass_on(o):
        far(o).wait_recv()
        near(o).start()

    loop(1, chips, pass_on)
    near(0).wait_recv()
    loop(1, chips, lambda o: near(o).wait_recv())
    loads[3].wait()
    loads[1].wait()

    where = [jnp.maximum(pos_ref[k], 0) for k in range(slots)]
    trow = [w // C for w in where]
    live = [[keep_ref[v, k] * (pos_ref[k] >= 0).astype(jnp.int32) for k in range(slots)] for v in range(2)]
    for k in range(slots):
        xcat[k * 128 : (k + 1) * 128, :] = xg[lax.rem(where[k], C)]

    def part_copy(o):
        return copy(pbuf.at[o], rbuf.at[o], p_send.at[o], p_recv.at[o], at_row(o), me_c)

    def part(o):
        t = at_row(o)
        out = []
        for v in range(2):
            lhs = []
            for k in range(slots):
                use = jnp.where(trow[k] == t, live[v][k], 0).astype(F32)
                lhs.append(tiles[k] * jnp.full((1, 128), use, F32).astype(BF16))
            out.append(jnp.dot(jnp.concatenate(lhs, axis=1), xcat[...], preferred_element_type=F32).astype(BF16))
        return out

    def part_send(o):
        first, second = part(o)
        pbuf[o, 0] = first
        pbuf[o, 1] = second
        part_copy(o).start()

    loop(1, R, part_send)
    mine = part(0)
    pbuf[0, 0] = mine[0]
    pbuf[0, 1] = mine[1]
    for i in range(turns):
        count_rows(i, tall, spread_ref, cnt)
    loads[2].wait()
    loop(1, R, lambda o: part_copy(o).wait_recv())

    for v in range(2):
        total = pbuf[0, v].astype(F32)
        if R <= 8:
            for o in range(1, R):
                total = total + rbuf[o, v].astype(F32)
        else:
            total = lax.fori_loop(1, R, lambda o, acc: acc + rbuf[o, v].astype(F32), total)
        total = total * fkeep[v : v + 1, :].astype(F32)
        gbuf[me_r, v] = total.astype(BF16)

    def agg_copy(o):
        return copy(gbuf.at[me_r], gbuf.at[me_r], g_send.at[o], g_recv.at[o], at_row(o), me_c)

    loop(1, R, lambda o: agg_copy(o).start())

    def embed(r):
        for v in range(2):
            z = jnp.dot(gbuf[r, v], weight[...], preferred_element_type=F32)
            scale = lax.rsqrt(jnp.sum(z * z, -1, keepdims=True) + eps)
            emb = z * scale
            rinv[r, v] = scale
            embf[r, v] = emb
            embb[r, v] = emb.astype(BF16)

    embed(me_r)
    h1 = embb[me_r, 0]
    h2 = embb[me_r, 1]
    h1f = h1.astype(F32)
    h2f = h2.astype(F32)
    pos = jnp.sum(h1f * h2f, -1, keepdims=True) / tau
    NT = (((1,), (1,)), ((), ()))
    TN = (((0,), (0,)), ((), ()))

    def scores(r):
        cols = pl.ds(pl.multiple_of(r * 128, 128), 128)
        counts = cnt[:, cols]
        s12 = lax.dot_general(h1, embb[r, 1], NT, preferred_element_type=F32) / tau
        s21 = lax.dot_general(h2, embb[r, 0], NT, preferred_element_type=F32) / tau
        eb[r, 0] = counts * jnp.exp(s12)
        eb[r, 1] = counts * jnp.exp(s21)

    scores(me_r)

    def arrived(o):
        r = from_row(o)
        agg_copy(o).wait_recv()
        embed(r)
        scores(r)

    loop(1, R, arrived)

    def row_sum(v):
        if R <= 8:
            total = eb[0, v]
            for r in range(1, R):
                total = total + eb[r, v]
        else:
            total = lax.fori_loop(1, R, lambda r, acc: acc + eb[r, v], eb[0, v])
        return jnp.sum(total, 1, keepdims=True)

    epos = jnp.exp(pos)
    tot1 = epos + row_sum(0)
    tot2 = epos + row_sum(1)
    loss = 0.5 * (jnp.log(tot1) - pos + (jnp.log(tot2) - pos))
    loss_out[...] = jnp.broadcast_to(loss, (nodes, 128)).T[0:1, :]
    both = epos / tot1 + epos / tot2 - 2.0
    coef = 1.0 / (2.0 * tau * float(R * C * nodes) ** 0.5)

    def dz_term(r, d_one, d_two):
        parts = []
        for v, d in enumerate((d_one, d_two)):
            emb = embf[r, v]
            dz = (d - emb * jnp.sum(emb * d, -1, keepdims=True)) * rinv[r, v]
            high = dz.astype(BF16)
            low = (dz - high.astype(F32)).astype(BF16)
            parts.append(jnp.concatenate([high, low], axis=1))
        rhs = jnp.concatenate(parts, axis=0)
        lhs = jnp.concatenate([gbuf[r, 0], gbuf[r, 1]], axis=0)
        return lax.dot_general(lhs, rhs, TN, preferred_element_type=F32)

    def weights(r):
        q1 = (eb[r, 0] / tot1).astype(BF16)
        q2 = (eb[r, 1] / tot2).astype(BF16)
        fore1 = jnp.dot(q1, embb[r, 1], preferred_element_type=F32)
        fore2 = jnp.dot(q2, embb[r, 0], preferred_element_type=F32)
        back1 = lax.dot_general(q2, h2, TN, preferred_element_type=F32)
        back2 = lax.dot_general(q1, h1, TN, preferred_element_type=F32)
        return fore1, fore2, back1, back2

    acc1, acc2, own1, own2 = weights(me_r)
    wacc[...] = jnp.zeros_like(wacc)

    def other(o, carry):
        r = from_row(o)
        fore1, fore2, back1, back2 = weights(r)
        wacc[...] += dz_term(r, coef * back1, coef * back2)
        return carry[0] + fore1, carry[1] + fore2

    if R <= 8:
        for o in range(1, R):
            acc1, acc2 = other(o, (acc1, acc2))
    else:
        acc1, acc2 = lax.fori_loop(1, R, other, (acc1, acc2))
    both_terms = wacc[...] + dz_term(
        me_r, coef * (both * h2f + acc1 + own1), coef * (both * h1f + acc2 + own2)
    )
    if wbuf.shape[0] > width:
        wbuf[...] = jnp.zeros_like(wbuf)
    wbuf[0:width, :] = both_terms[:, :width] + both_terms[:, width:]

    def a_copy(o):
        rows = pl.ds(pl.multiple_of(at_row(o) * cr, 8), cr)
        return copy(wbuf.at[rows, :], wr.at[o], a_send.at[o], a_recv.at[o], at_row(o), me_c)

    loop(1, R, lambda o: a_copy(o).start())
    own = wbuf[pl.ds(pl.multiple_of(me_r * cr, 8), cr), :]
    if ws.shape[0] > cr:
        ws[...] = jnp.zeros_like(ws)
    loop(1, R, lambda o: a_copy(o).wait_recv())
    if R <= 8:
        for o in range(1, R):
            own = own + wr[o]
    else:
        own = lax.fori_loop(1, R, lambda o, acc: acc + wr[o], own)
    ws[0:cr, :] = own

    def b_copy(o):
        rows = pl.ds(pl.multiple_of(at_col(o) * cc, 8), cc)
        return copy(ws.at[rows, :], wc.at[o], b_send.at[o], b_recv.at[o], me_r, at_col(o))

    loop(1, C, lambda o: b_copy(o).start())
    piece = ws[pl.ds(pl.multiple_of(me_c * cc, 8), cc), :]
    loop(1, C, lambda o: b_copy(o).wait_recv())
    if C <= 8:
        for o in range(1, C):
            piece = piece + wc[o]
    else:
        piece = lax.fori_loop(1, C, lambda o, acc: acc + wc[o], piece)
    mine_rows = pl.ds(pl.multiple_of(me_c * cc, 8), cc)
    wd[mine_rows, :] = piece

    def c_copy(o):
        return copy(wd.at[mine_rows, :], wd.at[mine_rows, :], c_send.at[o], c_recv.at[o], me_r, at_col(o))

    loop(1, C, lambda o: c_copy(o).start())
    loop(1, C, lambda o: c_copy(o).wait_recv())
    my_out = pl.ds(pl.multiple_of(me_r * cr, 8), cr)

    def d_copy(o):
        return copy(wd.at[pl.ds(0, cr), :], obuf.at[my_out, :], d_send.at[o], d_recv.at[o], at_row(o), me_c)

    loop(1, R, lambda o: d_copy(o).start())
    obuf[my_out, :] = wd[0:cr, :]
    loop(1, R, lambda o: d_copy(o).wait_recv())
    grad_out[...] = obuf[0:width, :]

    loop(1, chips, lambda o: far(o).wait_send())
    near(0).wait_send()
    loop(1, chips, lambda o: near(o).wait_send())
    loop(1, R, lambda o: part_copy(o).wait_send())
    loop(1, R, lambda o: agg_copy(o).wait_send())
    loop(1, R, lambda o: a_copy(o).wait_send())
    loop(1, C, lambda o: b_copy(o).wait_send())
    loop(1, C, lambda o: c_copy(o).wait_send())
    loop(1, R, lambda o: d_copy(o).wait_send())


def up(n, d, unit):
    return -(-(-(-n // d)) // unit) * unit


def shards(features, weight, tiles, tile_pos, edge_keep, feature_keep, negatives):
    nodes, width = features.shape
    slots = tiles.shape[0]
    R = lax.axis_size("row")
    C = lax.axis_size("col")
    group = R * nodes
    chips = C // 2
    cr = up(width, R, 8)
    cc = up(cr, C, 8)
    vmem = pl.BlockSpec(memory_space=pltpu.VMEM)
    held = pl.BlockSpec(memory_space=pl.ANY)
    smem = pl.BlockSpec(memory_space=pltpu.SMEM)
    sem = pltpu.SemaphoreType.DMA
    loss, grad = pl.pallas_call(
        functools.partial(step_kernel, R, C),
        out_shape=(
            jax.ShapeDtypeStruct((1, nodes), F32),
            jax.ShapeDtypeStruct((width, width), F32),
        ),
        in_specs=[held, held, held, smem, smem, vmem, held],
        out_specs=(vmem, vmem),
        scratch_shapes=[
            pltpu.VMEM(weight.shape, BF16),
            pltpu.VMEM(tiles.shape, BF16),
            pltpu.VMEM(negatives.shape, jnp.int32),
            pltpu.VMEM((negatives.shape[1], negatives.shape[1]), BF16),
            pltpu.VMEM(negatives.shape, jnp.int32),
            pltpu.VMEM((nodes, group), F32),
            pltpu.VMEM((C, nodes, width), BF16),
            pltpu.VMEM((slots * 128, width), BF16),
            pltpu.VMEM((R, 2, nodes, width), BF16),
            pltpu.VMEM((R, 2, nodes, width), BF16),
            pltpu.VMEM((R, 2, nodes, width), BF16),
            pltpu.VMEM((R, 2, nodes, width), F32),
            pltpu.VMEM((R, 2, nodes, width), BF16),
            pltpu.VMEM((R, 2, nodes, 1), F32),
            pltpu.VMEM((R, 2, nodes, 128), F32),
            pltpu.VMEM((width, 2 * width), F32),
            pltpu.VMEM((R * cr, width), F32),
            pltpu.VMEM((R, cr, width), F32),
            pltpu.VMEM((C * cc, width), F32),
            pltpu.VMEM((C, cc, width), F32),
            pltpu.VMEM((C * cc, width), F32),
            pltpu.VMEM((R * cr, width), F32),
            sem((chips,)), sem((chips,)), sem((chips,)), sem((chips,)),
            sem((R,)), sem((R,)), sem((R,)), sem((R,)),
            sem((R,)), sem((R,)), sem((C,)), sem((C,)),
            sem((C,)), sem((C,)), sem((R,)), sem((R,)), sem((4,)),
        ],
        compiler_params=pltpu.CompilerParams(
            collective_id=0, has_side_effects=True, vmem_limit_bytes=48 << 20
        ),
    )(features, weight, tiles, tile_pos, edge_keep, feature_keep, negatives)
    return loss.reshape(nodes), grad


def solution(mesh):
    in_specs = (
        P(("row", "col"), None),
        P(),
        P(("row", "col"), None, None),
        P(("row", "col")),
        P(None, ("row", "col")),
        P(),
        P(("row", "col"), None),
    )
    out_specs = (P(("row", "col")), P())
    return jax.shard_map(shards, mesh=mesh, in_specs=in_specs, out_specs=out_specs, check_vma=False)
```

```python
import functools

import jax
import jax.numpy as jnp
from jax import lax
from jax.experimental import pallas as pl
from jax.experimental.pallas import tpu as pltpu
from jax.sharding import PartitionSpec as P

tau = 0.5
eps = 1e-06
F32 = jnp.float32
BF16 = jnp.bfloat16
MESH = pl.DeviceIdType.MESH


def loop(start, stop, body):
    if stop - start <= 8:
        for i in range(start, stop):
            body(i)
    else:
        def step(i, carry):
            body(i)
            return carry
        lax.fori_loop(start, stop, step, 0)


def spread_matrix(ref):
    n = ref.shape[0]
    stride = n // 128
    row = lax.broadcasted_iota(jnp.int32, (128, 128), 0)
    lane = lax.broadcasted_iota(jnp.int32, (128, 128), 1)
    for k in range(n // 128):
        here = lane == row // stride + k * (128 // stride)
        for s in range(stride):
            hit = jnp.logical_and(here, row % stride == s)
            ref[k * 128 : (k + 1) * 128, s * 128 : (s + 1) * 128] = jnp.where(hit, 1.0, 0.0).astype(BF16)


def spread(neg, matrix, out):
    low = (neg[...] & 255).astype(F32).astype(BF16)
    high = (neg[...] >> 8).astype(F32).astype(BF16)
    nodes = neg.shape[0]
    both = jnp.dot(jnp.concatenate([low, high], axis=0), matrix[...], preferred_element_type=F32)
    out[...] = (both[:nodes] + 256.0 * both[nodes:]).astype(jnp.int32)


def count_rows(i, tall, spread_ref, cnt):
    stride = spread_ref.shape[1] // 128
    blocks = cnt.shape[1] // 128
    per = 4 if blocks % 4 == 0 else 1
    rows = pl.ds(pl.multiple_of(i * tall, 8), tall)
    lane = lax.broadcasted_iota(jnp.int32, (tall, 128), 1)

    def take(part, index):
        return jnp.take_along_axis(part, index, axis=1, mode="promise_in_bounds")

    def block_step(g, before):
        starts = [pl.multiple_of((g * per + j) * 128, 128) for j in range(per)]
        targets = [lane + at for at in starts]
        last = spread_ref[rows, (stride - 1) * 128 : stride * 128]
        lows = [jnp.zeros((tall, 128), jnp.int32)] * per
        for step in (64, 32, 16, 8, 4, 2, 1):
            seen = [take(last, low + (step - 1)) for low in lows]
            lows = [jnp.where(x <= t, low + step, low) for x, t, low in zip(seen, targets, lows)]
        ranks = [low * stride for low in lows]
        for s in range(stride):
            part = spread_ref[rows, s * 128 : (s + 1) * 128]
            seen = [take(part, low) for low in lows]
            ranks = [jnp.where(x <= t, k + 1, k) for x, t, k in zip(seen, targets, ranks)]
        for at, now in zip(starts, ranks):
            rolled = pltpu.roll(now, 1, 1)
            cnt[rows, pl.ds(at, 128)] = (now - jnp.where(lane == 0, before, rolled)).astype(F32)
            before = rolled
        return before

    first = jnp.zeros((tall, 128), jnp.int32)
    if blocks == per:
        block_step(0, first)
    else:
        lax.fori_loop(0, blocks // per, block_step, first)


def step_kernel(
    R, C,
    feat, weight_in, tiles_in, pos_ref, keep_ref, fkeep, neg_in,
    loss_out, grad_out,
    weight, tiles, neg, matrix, spread_ref, cnt,
    xg, prod, pbuf, rbuf, gbuf, embf, embb, rinv, eb, wacc, wbuf, wr, ws, wc, wd, obuf,
    f_send, f_recv, s_send, s_recv, p_send, p_recv, g_send, g_recv,
    a_send, a_recv, b_send, b_recv, c_send, c_recv, d_send, d_recv, l_sem,
):
    nodes, width = feat.shape
    halves = width // 128
    slots = tiles.shape[0]
    chips = C // 2
    cr = wr.shape[1]
    cc = wc.shape[1]
    me_r = lax.axis_index("row")
    me_c = lax.axis_index("col")
    chip = me_c // 2
    core = me_c % 2
    sib = chip * 2 + (1 - core)

    def at_row(o):
        return lax.rem(me_r + o, R)

    def from_row(o):
        return lax.rem(me_r + R - o, R)

    def at_col(o):
        return lax.rem(me_c + o, C)

    def from_col(o):
        return lax.rem(me_c + C - o, C)

    def copy(src, dst, send, recv, r, c):
        return pltpu.make_async_remote_copy(
            src_ref=src, dst_ref=dst, send_sem=send, recv_sem=recv,
            device_id=(r, c), device_id_type=MESH,
        )

    loads = [
        pltpu.make_async_copy(neg_in, neg, l_sem.at[0]),
        pltpu.make_async_copy(tiles_in, tiles, l_sem.at[1]),
        pltpu.make_async_copy(weight_in, weight, l_sem.at[2]),
    ]
    for h in range(halves):
        loads.append(pltpu.make_async_copy(feat.at[:, h * 128 : (h + 1) * 128], xg[h].at[me_c], l_sem.at[3 + h]))
    for load in loads:
        load.start()

    barrier = pltpu.get_barrier_semaphore()
    loop(1, R, lambda o: pl.semaphore_signal(barrier, inc=1, device_id=(at_row(o), me_c), device_id_type=MESH))
    loop(1, C, lambda o: pl.semaphore_signal(barrier, inc=1, device_id=(me_r, at_col(o)), device_id_type=MESH))
    pl.semaphore_wait(barrier, R + C - 2)

    def far(h, o):
        to = lax.rem(chip + o, chips) * 2 + core
        return copy(feat.at[:, h * 128 : (h + 1) * 128], xg[h].at[me_c], f_send.at[h, o], f_recv.at[h, o], me_r, to)

    def near(h, o):
        if isinstance(o, int) and o == 0:
            return copy(feat.at[:, h * 128 : (h + 1) * 128], xg[h].at[me_c], s_send.at[h, 0], s_recv.at[h, 0], me_r, sib)
        slot = lax.rem(chip + chips - o, chips) * 2 + core
        return copy(xg[h].at[slot], xg[h].at[slot], s_send.at[h, o], s_recv.at[h, o], me_r, sib)

    for h in range(halves):
        loop(1, chips, lambda o: far(h, o).start())
        near(h, 0).start()
    spread_matrix(matrix)
    loads[0].wait()
    spread(neg, matrix, spread_ref)
    tall = 32
    turns = nodes // tall
    for i in range(turns // 2):
        count_rows(i, tall, spread_ref, cnt)

    where = [jnp.maximum(pos_ref[k], 0) for k in range(slots)]
    trow = [w // C for w in where]
    live = [[keep_ref[v, k] * (pos_ref[k] >= 0).astype(jnp.int32) for k in range(slots)] for v in range(2)]

    def part_copy(h, o):
        return copy(pbuf.at[h, o], rbuf.at[h, o], p_send.at[h, o], p_recv.at[h, o], at_row(o), me_c)

    def part(h, o):
        t = at_row(o)
        here = [trow[k] == t for k in range(slots)]
        for v in range(2):
            total = None
            for k in range(slots):
                term = prod[k] * jnp.where(here[k], live[v][k], 0).astype(F32)
                total = term if total is None else total + term
            pbuf[h, o, v] = total.astype(BF16)

    for h in range(halves):
        def pass_on(o):
            far(h, o).wait_recv()
            near(h, o).start()

        loop(1, chips, pass_on)
        near(h, 0).wait_recv()
        loop(1, chips, lambda o: near(h, o).wait_recv())
        loads[3 + h].wait()
        if h == 0:
            loads[1].wait()
        for k in range(slots):
            prod[k] = jnp.dot(tiles[k], xg[h][lax.rem(where[k], C)], preferred_element_type=F32)

        def part_send(o):
            part(h, o)
            part_copy(h, o).start()

        loop(1, R, part_send)
        part(h, 0)

    def agg_copy(h, o):
        ref = gbuf.at[me_r, :, :, h * 128 : (h + 1) * 128]
        return copy(ref, ref, g_send.at[h, o], g_recv.at[h, o], at_row(o), me_c)

    for h in range(halves):
        loop(1, R, lambda o: part_copy(h, o).wait_recv())
        for v in range(2):
            total = pbuf[h, 0, v].astype(F32)
            if R <= 8:
                for o in range(1, R):
                    total = total + rbuf[h, o, v].astype(F32)
            else:
                total = lax.fori_loop(1, R, lambda o, acc: acc + rbuf[h, o, v].astype(F32), total)
            total = total * fkeep[v : v + 1, h * 128 : (h + 1) * 128].astype(F32)
            gbuf[me_r, v, :, h * 128 : (h + 1) * 128] = total.astype(BF16)
        loop(1, R, lambda o: agg_copy(h, o).start())
    for i in range(turns // 2, turns):
        count_rows(i, tall, spread_ref, cnt)
    loads[2].wait()

    def embed(r):
        for v in range(2):
            z = jnp.dot(gbuf[r, v], weight[...], preferred_element_type=F32)
            scale = lax.rsqrt(jnp.sum(z * z, -1, keepdims=True) + eps)
            emb = z * scale
            rinv[r, v] = scale
            embf[r, v] = emb
            embb[r, v] = emb.astype(BF16)

    embed(me_r)
    h1 = embb[me_r, 0]
    h2 = embb[me_r, 1]
    h1f = h1.astype(F32)
    h2f = h2.astype(F32)
    pos = jnp.sum(h1f * h2f, -1, keepdims=True) / tau
    NT = (((1,), (1,)), ((), ()))
    TN = (((0,), (0,)), ((), ()))

    def scores(r):
        cols = pl.ds(pl.multiple_of(r * 128, 128), 128)
        counts = cnt[:, cols]
        s12 = lax.dot_general(h1, embb[r, 1], NT, preferred_element_type=F32) / tau
        s21 = lax.dot_general(h2, embb[r, 0], NT, preferred_element_type=F32) / tau
        eb[r, 0] = counts * jnp.exp(s12)
        eb[r, 1] = counts * jnp.exp(s21)

    scores(me_r)

    def arrived(o):
        r = from_row(o)
        for h in range(halves):
            agg_copy(h, o).wait_recv()
        embed(r)
        scores(r)

    loop(1, R, arrived)

    def row_sum(v):
        if R <= 8:
            total = eb[0, v]
            for r in range(1, R):
                total = total + eb[r, v]
        else:
            total = lax.fori_loop(1, R, lambda r, acc: acc + eb[r, v], eb[0, v])
        return jnp.sum(total, 1, keepdims=True)

    epos = jnp.exp(pos)
    tot1 = epos + row_sum(0)
    tot2 = epos + row_sum(1)
    loss = 0.5 * (jnp.log(tot1) - pos + (jnp.log(tot2) - pos))
    loss_out[...] = jnp.broadcast_to(loss, (nodes, 128)).T[0]
    both = epos / tot1 + epos / tot2 - 2.0
    coef = 1.0 / (2.0 * tau * float(R * C * nodes) ** 0.5)

    def dz_term(r, d_one, d_two):
        parts = []
        for v, d in enumerate((d_one, d_two)):
            emb = embf[r, v]
            dz = (d - emb * jnp.sum(emb * d, -1, keepdims=True)) * rinv[r, v]
            high = dz.astype(BF16)
            low = (dz - high.astype(F32)).astype(BF16)
            parts.append(jnp.concatenate([high, low], axis=1))
        rhs = jnp.concatenate(parts, axis=0)
        lhs = jnp.concatenate([gbuf[r, 0], gbuf[r, 1]], axis=0)
        return lax.dot_general(lhs, rhs, TN, preferred_element_type=F32)

    def weights(r):
        q1 = (eb[r, 0] / tot1).astype(BF16)
        q2 = (eb[r, 1] / tot2).astype(BF16)
        fore1 = jnp.dot(q1, embb[r, 1], preferred_element_type=F32)
        fore2 = jnp.dot(q2, embb[r, 0], preferred_element_type=F32)
        back1 = lax.dot_general(q2, h2, TN, preferred_element_type=F32)
        back2 = lax.dot_general(q1, h1, TN, preferred_element_type=F32)
        return fore1, fore2, back1, back2

    acc1, acc2, own1, own2 = weights(me_r)
    wacc[...] = jnp.zeros_like(wacc)

    def other(o, carry):
        r = from_row(o)
        fore1, fore2, back1, back2 = weights(r)
        wacc[...] += dz_term(r, coef * back1, coef * back2)
        return carry[0] + fore1, carry[1] + fore2

    if R <= 8:
        for o in range(1, R):
            acc1, acc2 = other(o, (acc1, acc2))
    else:
        acc1, acc2 = lax.fori_loop(1, R, other, (acc1, acc2))
    both_terms = wacc[...] + dz_term(
        me_r, coef * (both * h2f + acc1 + own1), coef * (both * h1f + acc2 + own2)
    )
    if wbuf.shape[0] > width:
        wbuf[...] = jnp.zeros_like(wbuf)
    wbuf[0:width, :] = both_terms[:, :width] + both_terms[:, width:]

    def a_copy(o):
        rows = pl.ds(pl.multiple_of(at_row(o) * cr, 8), cr)
        return copy(wbuf.at[rows, :], wr.at[o], a_send.at[o], a_recv.at[o], at_row(o), me_c)

    loop(1, R, lambda o: a_copy(o).start())
    own = wbuf[pl.ds(pl.multiple_of(me_r * cr, 8), cr), :]
    if ws.shape[0] > cr:
        ws[...] = jnp.zeros_like(ws)
    loop(1, R, lambda o: a_copy(o).wait_recv())
    if R <= 8:
        for o in range(1, R):
            own = own + wr[o]
    else:
        own = lax.fori_loop(1, R, lambda o, acc: acc + wr[o], own)
    ws[0:cr, :] = own

    def b_copy(o):
        rows = pl.ds(pl.multiple_of(at_col(o) * cc, 8), cc)
        return copy(ws.at[rows, :], wc.at[o], b_send.at[o], b_recv.at[o], me_r, at_col(o))

    loop(1, C, lambda o: b_copy(o).start())
    piece = ws[pl.ds(pl.multiple_of(me_c * cc, 8), cc), :]
    loop(1, C, lambda o: b_copy(o).wait_recv())
    if C <= 8:
        for o in range(1, C):
            piece = piece + wc[o]
    else:
        piece = lax.fori_loop(1, C, lambda o, acc: acc + wc[o], piece)
    mine_rows = pl.ds(pl.multiple_of(me_c * cc, 8), cc)
    wd[mine_rows, :] = piece

    def c_copy(o):
        return copy(wd.at[mine_rows, :], wd.at[mine_rows, :], c_send.at[o], c_recv.at[o], me_r, at_col(o))

    loop(1, C, lambda o: c_copy(o).start())
    loop(1, C, lambda o: c_copy(o).wait_recv())
    my_out = pl.ds(pl.multiple_of(me_r * cr, 8), cr)

    def d_copy(o):
        return copy(wd.at[pl.ds(0, cr), :], obuf.at[my_out, :], d_send.at[o], d_recv.at[o], at_row(o), me_c)

    loop(1, R, lambda o: d_copy(o).start())
    obuf[my_out, :] = wd[0:cr, :]
    loop(1, R, lambda o: d_copy(o).wait_recv())
    grad_out[...] = obuf[0:width, :]

    for h in range(halves):
        loop(1, chips, lambda o: far(h, o).wait_send())
        near(h, 0).wait_send()
        loop(1, chips, lambda o: near(h, o).wait_send())
        loop(1, R, lambda o: part_copy(h, o).wait_send())
        loop(1, R, lambda o: agg_copy(h, o).wait_send())
    loop(1, R, lambda o: a_copy(o).wait_send())
    loop(1, C, lambda o: b_copy(o).wait_send())
    loop(1, C, lambda o: c_copy(o).wait_send())
    loop(1, R, lambda o: d_copy(o).wait_send())


def up(n, d, unit):
    return -(-(-(-n // d)) // unit) * unit


def shards(features, weight, tiles, tile_pos, edge_keep, feature_keep, negatives):
    nodes, width = features.shape
    halves = width // 128
    slots = tiles.shape[0]
    R = lax.axis_size("row")
    C = lax.axis_size("col")
    group = R * nodes
    chips = C // 2
    cr = up(width, R, 8)
    cc = up(cr, C, 8)
    vmem = pl.BlockSpec(memory_space=pltpu.VMEM)
    held = pl.BlockSpec(memory_space=pl.ANY)
    smem = pl.BlockSpec(memory_space=pltpu.SMEM)
    sem = pltpu.SemaphoreType.DMA
    loss, grad = pl.pallas_call(
        functools.partial(step_kernel, R, C),
        out_shape=(
            jax.ShapeDtypeStruct((nodes,), F32),
            jax.ShapeDtypeStruct((width, width), F32),
        ),
        in_specs=[held, held, held, smem, smem, vmem, held],
        out_specs=(vmem, vmem),
        scratch_shapes=[
            pltpu.VMEM(weight.shape, BF16),
            pltpu.VMEM(tiles.shape, BF16),
            pltpu.VMEM(negatives.shape, jnp.int32),
            pltpu.VMEM((negatives.shape[1], negatives.shape[1]), BF16),
            pltpu.VMEM(negatives.shape, jnp.int32),
            pltpu.VMEM((nodes, group), F32),
            [pltpu.VMEM((C, nodes, 128), BF16)] * halves,
            pltpu.VMEM((slots, 128, 128), F32),
            pltpu.VMEM((halves, R, 2, nodes, 128), BF16),
            pltpu.VMEM((halves, R, 2, nodes, 128), BF16),
            pltpu.VMEM((R, 2, nodes, width), BF16),
            pltpu.VMEM((R, 2, nodes, width), F32),
            pltpu.VMEM((R, 2, nodes, width), BF16),
            pltpu.VMEM((R, 2, nodes, 1), F32),
            pltpu.VMEM((R, 2, nodes, 128), F32),
            pltpu.VMEM((width, 2 * width), F32),
            pltpu.VMEM((R * cr, width), F32),
            pltpu.VMEM((R, cr, width), F32),
            pltpu.VMEM((C * cc, width), F32),
            pltpu.VMEM((C, cc, width), F32),
            pltpu.VMEM((C * cc, width), F32),
            pltpu.VMEM((R * cr, width), F32),
            sem((halves, chips)), sem((halves, chips)), sem((halves, chips)), sem((halves, chips)),
            sem((halves, R)), sem((halves, R)), sem((halves, R)), sem((halves, R)),
            sem((R,)), sem((R,)), sem((C,)), sem((C,)),
            sem((C,)), sem((C,)), sem((R,)), sem((R,)), sem((3 + halves,)),
        ],
        compiler_params=pltpu.CompilerParams(
            collective_id=0, has_side_effects=True, vmem_limit_bytes=60 << 20
        ),
    )(features, weight, tiles, tile_pos, edge_keep, feature_keep, negatives)
    return loss, grad


def solution(mesh):
    in_specs = (
        P(("row", "col"), None),
        P(),
        P(("row", "col"), None, None),
        P(("row", "col")),
        P(None, ("row", "col")),
        P(),
        P(("row", "col"), None),
    )
    out_specs = (P(("row", "col")), P())
    return jax.shard_map(shards, mesh=mesh, in_specs=in_specs, out_specs=out_specs, check_vma=False)
```

```python
import functools

import jax
import jax.numpy as jnp
from jax import lax
from jax.experimental import pallas as pl
from jax.experimental.pallas import tpu as pltpu
from jax.sharding import PartitionSpec as P

tau = 0.5
eps = 1e-06
F32 = jnp.float32
BF16 = jnp.bfloat16
MESH = pl.DeviceIdType.MESH


def loop(start, stop, body):
    if stop - start <= 16:
        for i in range(start, stop):
            body(i)
    else:
        def step(i, carry):
            body(i)
            return carry
        lax.fori_loop(start, stop, step, 0)


def spread_matrix(ref):
    n = ref.shape[0]
    stride = n // 128
    row = lax.broadcasted_iota(jnp.int32, (128, 128), 0)
    lane = lax.broadcasted_iota(jnp.int32, (128, 128), 1)
    for k in range(n // 128):
        here = lane == row // stride + k * (128 // stride)
        for s in range(stride):
            hit = jnp.logical_and(here, row % stride == s)
            ref[k * 128 : (k + 1) * 128, s * 128 : (s + 1) * 128] = jnp.where(hit, 1.0, 0.0).astype(BF16)


def spread(neg, matrix, out):
    low = (neg[...] & 255).astype(F32).astype(BF16)
    high = (neg[...] >> 8).astype(F32).astype(BF16)
    nodes = neg.shape[0]
    both = jnp.dot(jnp.concatenate([low, high], axis=0), matrix[...], preferred_element_type=F32)
    out[...] = (both[:nodes] + 256.0 * both[nodes:]).astype(jnp.int32)


def count_rows(i, tall, spread_ref, cnt):
    stride = spread_ref.shape[1] // 128
    blocks = cnt.shape[1] // 128
    per = 4 if blocks % 4 == 0 else 1
    rows = pl.ds(pl.multiple_of(i * tall, 8), tall)
    lane = lax.broadcasted_iota(jnp.int32, (tall, 128), 1)

    def take(part, index):
        return jnp.take_along_axis(part, index, axis=1, mode="promise_in_bounds")

    def block_step(g, before):
        starts = [pl.multiple_of((g * per + j) * 128, 128) for j in range(per)]
        targets = [lane + at for at in starts]
        last = spread_ref[rows, (stride - 1) * 128 : stride * 128]
        lows = [jnp.zeros((tall, 128), jnp.int32)] * per
        for step in (64, 32, 16, 8, 4, 2, 1):
            seen = [take(last, low + (step - 1)) for low in lows]
            lows = [jnp.where(x <= t, low + step, low) for x, t, low in zip(seen, targets, lows)]
        ranks = [low * stride for low in lows]
        for s in range(stride):
            part = spread_ref[rows, s * 128 : (s + 1) * 128]
            seen = [take(part, low) for low in lows]
            ranks = [jnp.where(x <= t, k + 1, k) for x, t, k in zip(seen, targets, ranks)]
        for at, now in zip(starts, ranks):
            rolled = pltpu.roll(now, 1, 1)
            cnt[rows, pl.ds(at, 128)] = (now - jnp.where(lane == 0, before, rolled)).astype(F32)
            before = rolled
        return before

    first = jnp.zeros((tall, 128), jnp.int32)
    if blocks == per:
        block_step(0, first)
    else:
        lax.fori_loop(0, blocks // per, block_step, first)


def step_kernel(
    R, C,
    feat, weight_in, tiles_in, pos_in, keep_in, fkeep_in, neg_in,
    loss_out, grad_out,
    weight, tiles, pos_ref, keep_ref, fkeep, neg, matrix, spread_ref, cnt,
    xg, prod, pbuf, rbuf, gbuf, embf, embb, rinv, eb, turned, dzb, wbuf, wsib, whalf, wr, obuf,
    f_send, f_recv, s_send, s_recv, p_send, p_recv, g_send, g_recv,
    a_send, a_recv, b_send, b_recv, c_send, c_recv, d_send, d_recv, l_sem,
):
    nodes, width = feat.shape
    halves = width // 128
    slots = tiles.shape[0]
    chips = C // 2
    peers = R * chips
    piece_rows = wr.shape[1]
    me_r = lax.axis_index("row")
    me_c = lax.axis_index("col")
    chip = me_c // 2
    core = me_c % 2
    sib = chip * 2 + (1 - core)

    def at_row(o):
        return lax.rem(me_r + o, R)

    def from_row(o):
        return lax.rem(me_r + R - o, R)

    index = me_r * chips + chip

    def at_peer(o):
        to = lax.rem(index + o, peers)
        return to // chips, lax.rem(to, chips) * 2 + core

    def copy(src, dst, send, recv, r, c):
        return pltpu.make_async_remote_copy(
            src_ref=src, dst_ref=dst, send_sem=send, recv_sem=recv,
            device_id=(r, c), device_id_type=MESH,
        )

    loads = [
        pltpu.make_async_copy(neg_in, neg, l_sem.at[0]),
        pltpu.make_async_copy(tiles_in, tiles, l_sem.at[1]),
        pltpu.make_async_copy(weight_in, weight, l_sem.at[2]),
    ]
    for h in range(halves):
        loads.append(pltpu.make_async_copy(feat.at[:, h * 128 : (h + 1) * 128], xg[h].at[me_c], l_sem.at[3 + h]))
    loads.append(pltpu.make_async_copy(pos_in, pos_ref, l_sem.at[3 + halves]))
    loads.append(pltpu.make_async_copy(keep_in, keep_ref, l_sem.at[4 + halves]))
    loads.append(pltpu.make_async_copy(fkeep_in, fkeep, l_sem.at[5 + halves]))
    for load in loads:
        load.start()

    barrier = pltpu.get_barrier_semaphore()
    loop(1, peers, lambda o: pl.semaphore_signal(barrier, inc=1, device_id=at_peer(o), device_id_type=MESH))
    pl.semaphore_signal(barrier, inc=1, device_id=(me_r, sib), device_id_type=MESH)
    pl.semaphore_wait(barrier, peers)

    def far(h, o):
        to = lax.rem(chip + o, chips) * 2 + core
        return copy(feat.at[:, h * 128 : (h + 1) * 128], xg[h].at[me_c], f_send.at[h, o], f_recv.at[h, o], me_r, to)

    def near(h, o):
        if isinstance(o, int) and o == 0:
            return copy(feat.at[:, h * 128 : (h + 1) * 128], xg[h].at[me_c], s_send.at[h, 0], s_recv.at[h, 0], me_r, sib)
        slot = lax.rem(chip + chips - o, chips) * 2 + core
        return copy(xg[h].at[slot], xg[h].at[slot], s_send.at[h, o], s_recv.at[h, o], me_r, sib)

    for h in range(halves):
        loop(1, chips, lambda o: far(h, o).start())
        near(h, 0).start()
    spread_matrix(matrix)
    loads[0].wait()
    spread(neg, matrix, spread_ref)
    tall = 32
    turns = nodes // tall
    for i in range(turns // 2):
        count_rows(i, tall, spread_ref, cnt)

    for load in loads[3 + halves :]:
        load.wait()
    where = [jnp.maximum(pos_ref[k], 0) for k in range(slots)]
    trow = [w // C for w in where]
    live = [[keep_ref[v, k] * (pos_ref[k] >= 0).astype(jnp.int32) for k in range(slots)] for v in range(2)]

    def part_copy(h, o):
        return copy(pbuf.at[h, o], rbuf.at[h, o], p_send.at[h, o], p_recv.at[h, o], at_row(o), me_c)

    def part(h, o):
        t = at_row(o)
        here = [trow[k] == t for k in range(slots)]
        for v in range(2):
            total = None
            for k in range(slots):
                term = prod[k] * jnp.where(here[k], live[v][k], 0).astype(F32)
                total = term if total is None else total + term
            pbuf[h, o, v] = total.astype(BF16)

    for h in range(halves):
        def pass_on(o):
            far(h, o).wait_recv()
            near(h, o).start()

        loop(1, chips, pass_on)
        near(h, 0).wait_recv()
        loop(1, chips, lambda o: near(h, o).wait_recv())
        loads[3 + h].wait()
        if h == 0:
            loads[1].wait()
        for k in range(slots):
            prod[k] = jnp.dot(tiles[k], xg[h][lax.rem(where[k], C)], preferred_element_type=F32)

        def part_send(o):
            part(h, o)
            part_copy(h, o).start()

        loop(1, R, part_send)
        part(h, 0)

    def agg_copy(h, o):
        ref = gbuf.at[me_r, :, :, h * 128 : (h + 1) * 128]
        return copy(ref, ref, g_send.at[h, o], g_recv.at[h, o], at_row(o), me_c)

    for h in range(halves):
        loop(1, R, lambda o: part_copy(h, o).wait_recv())
        for v in range(2):
            total = pbuf[h, 0, v].astype(F32)
            if R <= 8:
                for o in range(1, R):
                    total = total + rbuf[h, o, v].astype(F32)
            else:
                total = lax.fori_loop(1, R, lambda o, acc: acc + rbuf[h, o, v].astype(F32), total)
            total = total * fkeep[v : v + 1, h * 128 : (h + 1) * 128].astype(F32)
            gbuf[me_r, v, :, h * 128 : (h + 1) * 128] = total.astype(BF16)
        loop(1, R, lambda o: agg_copy(h, o).start())
    for i in range(turns // 2, turns):
        count_rows(i, tall, spread_ref, cnt)
    loads[2].wait()

    def embed(r):
        stacked = gbuf[r].reshape(2 * nodes, width)
        z = jnp.dot(stacked, weight[...], preferred_element_type=F32)
        scale = lax.rsqrt(jnp.sum(z * z, -1, keepdims=True) + eps)
        emb = z * scale
        rinv[r] = scale.reshape(2, nodes, 1)
        embf[r] = emb.reshape(2, nodes, width)
        embb[r] = emb.astype(BF16).reshape(2, nodes, width)
        turned[r] = stacked.T

    embed(me_r)
    h1 = embb[me_r, 0]
    h2 = embb[me_r, 1]
    h1f = h1.astype(F32)
    h2f = h2.astype(F32)
    pos = jnp.sum(h1f * h2f, -1, keepdims=True) / tau
    NT = (((1,), (1,)), ((), ()))
    TN = (((0,), (0,)), ((), ()))

    def scores(r):
        cols = pl.ds(pl.multiple_of(r * 128, 128), 128)
        counts = cnt[:, cols]
        s12 = lax.dot_general(h1, embb[r, 1], NT, preferred_element_type=F32) / tau
        s21 = lax.dot_general(h2, embb[r, 0], NT, preferred_element_type=F32) / tau
        eb[r, 0] = counts * jnp.exp(s12)
        eb[r, 1] = counts * jnp.exp(s21)

    scores(me_r)

    def arrived(o):
        r = from_row(o)
        for h in range(halves):
            agg_copy(h, o).wait_recv()
        embed(r)
        scores(r)

    loop(1, R, arrived)

    def row_sum(v):
        if R <= 8:
            total = eb[0, v]
            for r in range(1, R):
                total = total + eb[r, v]
        else:
            total = lax.fori_loop(1, R, lambda r, acc: acc + eb[r, v], eb[0, v])
        return jnp.sum(total, 1, keepdims=True)

    epos = jnp.exp(pos)
    tot1 = epos + row_sum(0)
    tot2 = epos + row_sum(1)
    loss = 0.5 * (jnp.log(tot1) - pos + (jnp.log(tot2) - pos))
    loss_out[...] = jnp.broadcast_to(loss, (nodes, 128)).T[0]
    both = epos / tot1 + epos / tot2 - 2.0
    coef = 1.0 / (2.0 * tau * float(R * C * nodes) ** 0.5)

    def dz_term(r, d_one, d_two):
        for v, d in enumerate((d_one, d_two)):
            emb = embf[r, v]
            dz = (d - emb * jnp.sum(emb * d, -1, keepdims=True)) * rinv[r, v]
            high = dz.astype(BF16)
            dzb[r, v * nodes : (v + 1) * nodes, :width] = high
            dzb[r, v * nodes : (v + 1) * nodes, width:] = (dz - high.astype(F32)).astype(BF16)

    def weights(r):
        q1 = (eb[r, 0] / tot1).astype(BF16)
        q2 = (eb[r, 1] / tot2).astype(BF16)
        fore1 = jnp.dot(q1, embb[r, 1], preferred_element_type=F32)
        fore2 = jnp.dot(q2, embb[r, 0], preferred_element_type=F32)
        back1 = lax.dot_general(q2, h2, TN, preferred_element_type=F32)
        back2 = lax.dot_general(q1, h1, TN, preferred_element_type=F32)
        return fore1, fore2, back1, back2

    acc1, acc2, own1, own2 = weights(me_r)

    def other(o, carry):
        r = from_row(o)
        fore1, fore2, back1, back2 = weights(r)
        dz_term(r, coef * back1, coef * back2)
        return carry[0] + fore1, carry[1] + fore2

    if R <= 8:
        for o in range(1, R):
            acc1, acc2 = other(o, (acc1, acc2))
    else:
        acc1, acc2 = lax.fori_loop(1, R, other, (acc1, acc2))
    dz_term(
        me_r, coef * (both * h2f + acc1 + own1), coef * (both * h1f + acc2 + own2)
    )

    def grad_term(r):
        return jnp.dot(turned[r], dzb[r], preferred_element_type=F32)

    if R <= 8:
        terms = grad_term(0)
        for r in range(1, R):
            terms = terms + grad_term(r)
    else:
        terms = lax.fori_loop(1, R, lambda r, acc: acc + grad_term(r), grad_term(0))
    wbuf[...] = terms[:, :width] + terms[:, width:]

    half = width // 2
    a_copy = copy(
        wbuf.at[pl.ds(pl.multiple_of((1 - core) * half, 8), half), :], wsib, a_send, a_recv, me_r, sib
    )
    a_copy.start()
    own = wbuf[pl.ds(pl.multiple_of(core * half, 8), half), :]
    if whalf.shape[0] > half:
        whalf[...] = jnp.zeros_like(whalf)
    a_copy.wait_recv()
    whalf[0:half, :] = own + wsib[...]

    def b_copy(o):
        to = lax.rem(index + o, peers)
        rows = pl.ds(pl.multiple_of(to * piece_rows, 8), piece_rows)
        r, c = at_peer(o)
        return copy(whalf.at[rows, :], wr.at[o], b_send.at[o], b_recv.at[o], r, c)

    loop(1, peers, lambda o: b_copy(o).start())
    my_rows = pl.ds(pl.multiple_of(index * piece_rows, 8), piece_rows)
    piece = whalf[my_rows, :]
    loop(1, peers, lambda o: b_copy(o).wait_recv())
    if peers <= 32:
        for o in range(1, peers):
            piece = piece + wr[o]
    else:
        piece = lax.fori_loop(1, peers, lambda o, acc: acc + wr[o], piece)
    obuf[core, my_rows, :] = piece

    def c_copy(o):
        r, c = at_peer(o)
        ref = obuf.at[core, my_rows, :]
        return copy(ref, ref, c_send.at[o], c_recv.at[o], r, c)

    loop(1, peers, lambda o: c_copy(o).start())
    loop(1, peers, lambda o: c_copy(o).wait_recv())
    mine_done = obuf.at[core, pl.ds(0, half), :]
    d_copy = copy(mine_done, mine_done, d_send, d_recv, me_r, sib)
    d_copy.start()
    my_half = pl.ds(pl.multiple_of(core * half, 8), half)
    grad_out[my_half, :] = obuf[core, 0:half, :]
    d_copy.wait_recv()
    its_half = pl.ds(pl.multiple_of((1 - core) * half, 8), half)
    grad_out[its_half, :] = obuf[1 - core, 0:half, :]

    for h in range(halves):
        loop(1, chips, lambda o: far(h, o).wait_send())
        near(h, 0).wait_send()
        loop(1, chips, lambda o: near(h, o).wait_send())
        loop(1, R, lambda o: part_copy(h, o).wait_send())
        loop(1, R, lambda o: agg_copy(h, o).wait_send())
    a_copy.wait_send()
    loop(1, peers, lambda o: b_copy(o).wait_send())
    loop(1, peers, lambda o: c_copy(o).wait_send())
    d_copy.wait_send()


def hand_over(loss, grad, loss_out, grad_out, sems):
    first = pltpu.make_async_copy(loss, loss_out, sems.at[0])
    second = pltpu.make_async_copy(grad, grad_out, sems.at[1])
    second.start()
    first.start()
    first.wait()
    second.wait()


def up(n, d, unit):
    return -(-(-(-n // d)) // unit) * unit


def shards(features, weight, tiles, tile_pos, edge_keep, feature_keep, negatives):
    nodes, width = features.shape
    halves = width // 128
    slots = tiles.shape[0]
    R = lax.axis_size("row")
    C = lax.axis_size("col")
    group = R * nodes
    chips = C // 2
    peers = R * chips
    piece_rows = up(width // 2, peers, 8)
    vmem = pl.BlockSpec(memory_space=pltpu.VMEM)
    held = pl.BlockSpec(memory_space=pl.ANY)
    sem = pltpu.SemaphoreType.DMA
    loss, grad = pl.pallas_call(
        functools.partial(step_kernel, R, C),
        out_shape=(
            jax.ShapeDtypeStruct((nodes,), F32),
            jax.ShapeDtypeStruct((width, width), F32),
        ),
        in_specs=[held] * 7,
        out_specs=(vmem, vmem),
        scratch_shapes=[
            pltpu.VMEM(weight.shape, BF16),
            pltpu.VMEM(tiles.shape, BF16),
            pltpu.SMEM(tile_pos.shape, jnp.int32),
            pltpu.SMEM(edge_keep.shape, jnp.int32),
            pltpu.VMEM(feature_keep.shape, jnp.int32),
            pltpu.VMEM(negatives.shape, jnp.int32),
            pltpu.VMEM((negatives.shape[1], negatives.shape[1]), BF16),
            pltpu.VMEM(negatives.shape, jnp.int32),
            pltpu.VMEM((nodes, group), F32),
            [pltpu.VMEM((C, nodes, 128), BF16)] * halves,
            pltpu.VMEM((slots, 128, 128), F32),
            pltpu.VMEM((halves, R, 2, nodes, 128), BF16),
            pltpu.VMEM((halves, R, 2, nodes, 128), BF16),
            pltpu.VMEM((R, 2, nodes, width), BF16),
            pltpu.VMEM((R, 2, nodes, width), F32),
            pltpu.VMEM((R, 2, nodes, width), BF16),
            pltpu.VMEM((R, 2, nodes, 1), F32),
            pltpu.VMEM((R, 2, nodes, 128), F32),
            pltpu.VMEM((R, width, 2 * nodes), BF16),
            pltpu.VMEM((R, 2 * nodes, 2 * width), BF16),
            pltpu.VMEM((width, width), F32),
            pltpu.VMEM((width // 2, width), F32),
            pltpu.VMEM((peers * piece_rows, width), F32),
            pltpu.VMEM((peers, piece_rows, width), F32),
            pltpu.VMEM((2, peers * piece_rows, width), F32),
            sem((halves, chips)), sem((halves, chips)), sem((halves, chips)), sem((halves, chips)),
            sem((halves, R)), sem((halves, R)), sem((halves, R)), sem((halves, R)),
            sem, sem, sem((peers,)), sem((peers,)),
            sem((peers,)), sem((peers,)), sem, sem, sem((6 + halves,)),
        ],
        compiler_params=pltpu.CompilerParams(
            collective_id=0, has_side_effects=True, vmem_limit_bytes=60 << 20
        ),
    )(features, weight, tiles, tile_pos, edge_keep, feature_keep, negatives)
    return pl.pallas_call(
        hand_over,
        out_shape=(
            jax.ShapeDtypeStruct((nodes,), F32),
            jax.ShapeDtypeStruct((width, width), F32),
        ),
        in_specs=[held] * 2,
        out_specs=(held, held),
        scratch_shapes=[sem((2,))],
        compiler_params=pltpu.CompilerParams(vmem_limit_bytes=60 << 20),
    )(loss, grad)


def solution(mesh):
    in_specs = (
        P(("row", "col"), None),
        P(),
        P(("row", "col"), None, None),
        P(("row", "col")),
        P(None, ("row", "col")),
        P(),
        P(("row", "col"), None),
    )
    out_specs = (P(("row", "col")), P())
    return jax.shard_map(shards, mesh=mesh, in_specs=in_specs, out_specs=out_specs, check_vma=False)
```

```python
import functools

import jax
import jax.numpy as jnp
from jax import lax
from jax.experimental import pallas as pl
from jax.experimental.pallas import tpu as pltpu
from jax.sharding import PartitionSpec as P

tau = 0.5
eps = 1e-06
F32 = jnp.float32
BF16 = jnp.bfloat16
MESH = pl.DeviceIdType.MESH


def loop(start, stop, body):
    if stop - start <= 16:
        for i in range(start, stop):
            body(i)
    else:
        def step(i, carry):
            body(i)
            return carry
        lax.fori_loop(start, stop, step, 0)


def spread_matrix(ref):
    n = ref.shape[0]
    stride = n // 128
    row = lax.broadcasted_iota(jnp.int32, (128, 128), 0)
    lane = lax.broadcasted_iota(jnp.int32, (128, 128), 1)
    for k in range(n // 128):
        here = lane == row // stride + k * (128 // stride)
        for s in range(stride):
            hit = jnp.logical_and(here, row % stride == s)
            ref[k * 128 : (k + 1) * 128, s * 128 : (s + 1) * 128] = jnp.where(hit, 1.0, 0.0).astype(BF16)


def spread(neg, matrix, out):
    low = (neg[...] & 255).astype(F32).astype(BF16)
    high = (neg[...] >> 8).astype(F32).astype(BF16)
    nodes = neg.shape[0]
    both = jnp.dot(jnp.concatenate([low, high], axis=0), matrix[...], preferred_element_type=F32)
    out[...] = (both[:nodes] + 256.0 * both[nodes:]).astype(jnp.int32)


def count_rows(i, tall, spread_ref, cnt):
    stride = spread_ref.shape[1] // 128
    blocks = cnt.shape[1] // 128
    per = 4 if blocks % 4 == 0 else 1
    rows = pl.ds(pl.multiple_of(i * tall, 8), tall)
    lane = lax.broadcasted_iota(jnp.int32, (tall, 128), 1)

    def take(part, index):
        return jnp.take_along_axis(part, index, axis=1, mode="promise_in_bounds")

    def block_step(g, before):
        starts = [pl.multiple_of((g * per + j) * 128, 128) for j in range(per)]
        targets = [lane + at for at in starts]
        last = spread_ref[rows, (stride - 1) * 128 : stride * 128]
        lows = [jnp.zeros((tall, 128), jnp.int32)] * per
        for step in (64, 32, 16, 8, 4, 2, 1):
            seen = [take(last, low + (step - 1)) for low in lows]
            lows = [jnp.where(x <= t, low + step, low) for x, t, low in zip(seen, targets, lows)]
        ranks = [low * stride for low in lows]
        for s in range(stride):
            part = spread_ref[rows, s * 128 : (s + 1) * 128]
            seen = [take(part, low) for low in lows]
            ranks = [jnp.where(x <= t, k + 1, k) for x, t, k in zip(seen, targets, ranks)]
        for at, now in zip(starts, ranks):
            rolled = pltpu.roll(now, 1, 1)
            cnt[rows, pl.ds(at, 128)] = (now - jnp.where(lane == 0, before, rolled)).astype(F32)
            before = rolled
        return before

    first = jnp.zeros((tall, 128), jnp.int32)
    if blocks == per:
        block_step(0, first)
    else:
        lax.fori_loop(0, blocks // per, block_step, first)


def step_kernel(
    R, C,
    feat, weight_in, tiles_in, pos_in, keep_in, fkeep_in, neg_in,
    loss_out, grad_out,
    weight, tiles, pos_ref, keep_ref, fkeep, neg, matrix, spread_ref, cnt,
    xg, prod, pbuf, rbuf, gbuf, embf, embb, rinv, eb, turned, dzb, wbuf, wsib, whalf, wr, obuf,
    f_send, f_recv, s_send, s_recv, p_send, p_recv, g_send, g_recv,
    a_send, a_recv, b_send, b_recv, c_send, c_recv, d_send, d_recv, l_sem,
):
    nodes, width = feat.shape
    halves = width // 128
    slots = tiles.shape[0]
    chips = C // 2
    peers = R * chips
    piece_rows = wr.shape[1]
    me_r = lax.axis_index("row")
    me_c = lax.axis_index("col")
    chip = me_c // 2
    core = me_c % 2
    sib = chip * 2 + (1 - core)

    def at_row(o):
        return lax.rem(me_r + o, R)

    def from_row(o):
        return lax.rem(me_r + R - o, R)

    index = me_r * chips + chip

    def at_peer(o):
        to = lax.rem(index + o, peers)
        return to // chips, lax.rem(to, chips) * 2 + core

    def copy(src, dst, send, recv, r, c):
        return pltpu.make_async_remote_copy(
            src_ref=src, dst_ref=dst, send_sem=send, recv_sem=recv,
            device_id=(r, c), device_id_type=MESH,
        )

    loads = [
        pltpu.make_async_copy(neg_in, neg, l_sem.at[0]),
        pltpu.make_async_copy(tiles_in, tiles, l_sem.at[1]),
        pltpu.make_async_copy(weight_in, weight, l_sem.at[2]),
    ]
    for h in range(halves):
        loads.append(pltpu.make_async_copy(feat.at[:, h * 128 : (h + 1) * 128], xg[h].at[me_c], l_sem.at[3 + h]))
    loads.append(pltpu.make_async_copy(pos_in, pos_ref, l_sem.at[3 + halves]))
    loads.append(pltpu.make_async_copy(keep_in, keep_ref, l_sem.at[4 + halves]))
    loads.append(pltpu.make_async_copy(fkeep_in, fkeep, l_sem.at[5 + halves]))
    for load in loads:
        load.start()

    barrier = pltpu.get_barrier_semaphore()
    loop(1, peers, lambda o: pl.semaphore_signal(barrier, inc=1, device_id=at_peer(o), device_id_type=MESH))
    pl.semaphore_signal(barrier, inc=1, device_id=(me_r, sib), device_id_type=MESH)
    spread_matrix(matrix)
    pl.semaphore_wait(barrier, peers)

    def far(h, o):
        to = lax.rem(chip + o, chips) * 2 + core
        return copy(feat.at[:, h * 128 : (h + 1) * 128], xg[h].at[me_c], f_send.at[h, o], f_recv.at[h, o], me_r, to)

    def near(h, o):
        if isinstance(o, int) and o == 0:
            return copy(feat.at[:, h * 128 : (h + 1) * 128], xg[h].at[me_c], s_send.at[h, 0], s_recv.at[h, 0], me_r, sib)
        slot = lax.rem(chip + chips - o, chips) * 2 + core
        return copy(xg[h].at[slot], xg[h].at[slot], s_send.at[h, o], s_recv.at[h, o], me_r, sib)

    for h in range(halves):
        loop(1, chips, lambda o: far(h, o).start())
        near(h, 0).start()
    loads[0].wait()
    spread(neg, matrix, spread_ref)
    tall = 32
    turns = nodes // tall
    for i in range(turns // 2):
        count_rows(i, tall, spread_ref, cnt)

    for load in loads[3 + halves :]:
        load.wait()
    where = [jnp.maximum(pos_ref[k], 0) for k in range(slots)]
    trow = [w // C for w in where]
    live = [[keep_ref[v, k] * (pos_ref[k] >= 0).astype(jnp.int32) for k in range(slots)] for v in range(2)]

    def part_copy(h, o):
        return copy(pbuf.at[h, o], rbuf.at[h, o], p_send.at[h, o], p_recv.at[h, o], at_row(o), me_c)

    def part(h, o):
        t = at_row(o)
        here = [trow[k] == t for k in range(slots)]
        for v in range(2):
            total = None
            for k in range(slots):
                term = prod[h, k] * jnp.where(here[k], live[v][k], 0).astype(F32)
                total = term if total is None else total + term
            pbuf[h, o, v] = total.astype(BF16)

    for h in range(halves):
        def pass_on(o):
            far(h, o).wait_recv()
            near(h, o).start()

        loop(1, chips, pass_on)
        near(h, 0).wait_recv()
        loop(1, chips, lambda o: near(h, o).wait_recv())
        loads[3 + h].wait()
        if h == 0:
            loads[1].wait()
        for k in range(slots):
            prod[h, k] = jnp.dot(tiles[k], xg[h][lax.rem(where[k], C)], preferred_element_type=F32)

        def part_send(o):
            part(h, o)
            part_copy(h, o).start()

        loop(1, R, part_send)

    def agg_copy(h, o):
        ref = gbuf.at[me_r, :, :, h * 128 : (h + 1) * 128]
        return copy(ref, ref, g_send.at[h, o], g_recv.at[h, o], at_row(o), me_c)

    for h in range(halves):
        part(h, 0)
        loop(1, R, lambda o: part_copy(h, o).wait_recv())
        for v in range(2):
            total = pbuf[h, 0, v].astype(F32)
            if R <= 8:
                for o in range(1, R):
                    total = total + rbuf[h, o, v].astype(F32)
            else:
                total = lax.fori_loop(1, R, lambda o, acc: acc + rbuf[h, o, v].astype(F32), total)
            total = total * fkeep[v : v + 1, h * 128 : (h + 1) * 128].astype(F32)
            gbuf[me_r, v, :, h * 128 : (h + 1) * 128] = total.astype(BF16)
        loop(1, R, lambda o: agg_copy(h, o).start())
    for i in range(turns // 2, turns):
        count_rows(i, tall, spread_ref, cnt)
    loads[2].wait()

    def embed(r):
        stacked = gbuf[r].reshape(2 * nodes, width)
        z = jnp.dot(stacked, weight[...], preferred_element_type=F32)
        scale = lax.rsqrt(jnp.sum(z * z, -1, keepdims=True) + eps)
        emb = z * scale
        rinv[r] = scale.reshape(2, nodes, 1)
        embf[r] = emb.reshape(2, nodes, width)
        embb[r] = emb.astype(BF16).reshape(2, nodes, width)
        turned[r] = stacked.T

    embed(me_r)
    h1 = embb[me_r, 0]
    h2 = embb[me_r, 1]
    h1f = h1.astype(F32)
    h2f = h2.astype(F32)
    pos = jnp.sum(h1f * h2f, -1, keepdims=True) / tau
    NT = (((1,), (1,)), ((), ()))
    TN = (((0,), (0,)), ((), ()))

    def scores(r):
        cols = pl.ds(pl.multiple_of(r * 128, 128), 128)
        counts = cnt[:, cols]
        s12 = lax.dot_general(h1, embb[r, 1], NT, preferred_element_type=F32) / tau
        s21 = lax.dot_general(h2, embb[r, 0], NT, preferred_element_type=F32) / tau
        eb[r, 0] = counts * jnp.exp(s12)
        eb[r, 1] = counts * jnp.exp(s21)

    scores(me_r)

    def arrived(o):
        r = from_row(o)
        for h in range(halves):
            agg_copy(h, o).wait_recv()
        embed(r)
        scores(r)

    loop(1, R, arrived)

    def row_sum(v):
        if R <= 8:
            total = eb[0, v]
            for r in range(1, R):
                total = total + eb[r, v]
        else:
            total = lax.fori_loop(1, R, lambda r, acc: acc + eb[r, v], eb[0, v])
        return jnp.sum(total, 1, keepdims=True)

    epos = jnp.exp(pos)
    tot1 = epos + row_sum(0)
    tot2 = epos + row_sum(1)
    loss = 0.5 * (jnp.log(tot1) - pos + (jnp.log(tot2) - pos))
    both = epos / tot1 + epos / tot2 - 2.0
    coef = 1.0 / (2.0 * tau * float(R * C * nodes) ** 0.5)

    def dz_term(r, d_one, d_two):
        for v, d in enumerate((d_one, d_two)):
            emb = embf[r, v]
            dz = (d - emb * jnp.sum(emb * d, -1, keepdims=True)) * rinv[r, v]
            high = dz.astype(BF16)
            dzb[r, v * nodes : (v + 1) * nodes, :width] = high
            dzb[r, v * nodes : (v + 1) * nodes, width:] = (dz - high.astype(F32)).astype(BF16)

    def weights(r):
        q1 = (eb[r, 0] / tot1).astype(BF16)
        q2 = (eb[r, 1] / tot2).astype(BF16)
        fore1 = jnp.dot(q1, embb[r, 1], preferred_element_type=F32)
        fore2 = jnp.dot(q2, embb[r, 0], preferred_element_type=F32)
        back1 = lax.dot_general(q2, h2, TN, preferred_element_type=F32)
        back2 = lax.dot_general(q1, h1, TN, preferred_element_type=F32)
        return fore1, fore2, back1, back2

    acc1, acc2, own1, own2 = weights(me_r)

    def other(o, carry):
        r = from_row(o)
        fore1, fore2, back1, back2 = weights(r)
        dz_term(r, coef * back1, coef * back2)
        return carry[0] + fore1, carry[1] + fore2

    if R <= 8:
        for o in range(1, R):
            acc1, acc2 = other(o, (acc1, acc2))
    else:
        acc1, acc2 = lax.fori_loop(1, R, other, (acc1, acc2))
    dz_term(
        me_r, coef * (both * h2f + acc1 + own1), coef * (both * h1f + acc2 + own2)
    )

    half = width // 2

    def grad_half(side):
        rows = pl.ds(pl.multiple_of(side * half, 16), half)

        def term(r):
            return jnp.dot(turned[r, rows, :], dzb[r], preferred_element_type=F32)

        if R <= 8:
            terms = term(0)
            for r in range(1, R):
                terms = terms + term(r)
        else:
            terms = lax.fori_loop(1, R, lambda r, acc: acc + term(r), term(0))
        return terms[:, :width] + terms[:, width:]

    wbuf[...] = grad_half(1 - core)
    a_copy = copy(wbuf, wsib, a_send, a_recv, me_r, sib)
    a_copy.start()
    own = grad_half(core)
    if whalf.shape[0] > half:
        whalf[...] = jnp.zeros_like(whalf)
    a_copy.wait_recv()
    whalf[0:half, :] = own + wsib[...]

    def b_copy(o):
        to = lax.rem(index + o, peers)
        rows = pl.ds(pl.multiple_of(to * piece_rows, 8), piece_rows)
        r, c = at_peer(o)
        return copy(whalf.at[rows, :], wr.at[o], b_send.at[o], b_recv.at[o], r, c)

    loop(1, peers, lambda o: b_copy(o).start())
    loss_out[...] = jnp.broadcast_to(loss, (nodes, 128)).T[0]
    my_rows = pl.ds(pl.multiple_of(index * piece_rows, 8), piece_rows)
    piece = whalf[my_rows, :]
    loop(1, peers, lambda o: b_copy(o).wait_recv())
    if peers <= 32:
        for o in range(1, peers):
            piece = piece + wr[o]
    else:
        piece = lax.fori_loop(1, peers, lambda o, acc: acc + wr[o], piece)
    obuf[core, my_rows, :] = piece

    def c_copy(o):
        r, c = at_peer(o)
        ref = obuf.at[core, my_rows, :]
        return copy(ref, ref, c_send.at[o], c_recv.at[o], r, c)

    loop(1, peers, lambda o: c_copy(o).start())
    loop(1, peers, lambda o: c_copy(o).wait_recv())
    mine_done = obuf.at[core, pl.ds(0, half), :]
    d_copy = copy(mine_done, mine_done, d_send, d_recv, me_r, sib)
    d_copy.start()
    my_half = pl.ds(pl.multiple_of(core * half, 8), half)
    grad_out[my_half, :] = obuf[core, 0:half, :]
    d_copy.wait_recv()
    its_half = pl.ds(pl.multiple_of((1 - core) * half, 8), half)
    grad_out[its_half, :] = obuf[1 - core, 0:half, :]

    for h in range(halves):
        loop(1, chips, lambda o: far(h, o).wait_send())
        near(h, 0).wait_send()
        loop(1, chips, lambda o: near(h, o).wait_send())
        loop(1, R, lambda o: part_copy(h, o).wait_send())
        loop(1, R, lambda o: agg_copy(h, o).wait_send())
    a_copy.wait_send()
    loop(1, peers, lambda o: b_copy(o).wait_send())
    loop(1, peers, lambda o: c_copy(o).wait_send())
    d_copy.wait_send()


def hand_over(loss, grad, loss_out, grad_out, loss_buf, grad_buf, in_sems, out_sems):
    chunks = out_sems.shape[0] - 1
    rows = grad.shape[0] // chunks
    ins = [pltpu.make_async_copy(loss, loss_buf, in_sems.at[chunks])]
    outs = [pltpu.make_async_copy(loss_buf, loss_out, out_sems.at[chunks])]
    for i in range(chunks):
        part = pl.ds(i * rows, rows)
        ins.append(pltpu.make_async_copy(grad.at[part, :], grad_buf.at[part, :], in_sems.at[i]))
        outs.append(pltpu.make_async_copy(grad_buf.at[part, :], grad_out.at[part, :], out_sems.at[i]))
    for move in ins:
        move.start()
    for move, then in zip(ins, outs):
        move.wait()
        then.start()
    for move in outs:
        move.wait()


def up(n, d, unit):
    return -(-(-(-n // d)) // unit) * unit


def shards(features, weight, tiles, tile_pos, edge_keep, feature_keep, negatives):
    nodes, width = features.shape
    halves = width // 128
    slots = tiles.shape[0]
    R = lax.axis_size("row")
    C = lax.axis_size("col")
    group = R * nodes
    chips = C // 2
    peers = R * chips
    piece_rows = up(width // 2, peers, 8)
    vmem = pl.BlockSpec(memory_space=pltpu.VMEM)
    held = pl.BlockSpec(memory_space=pl.ANY)
    sem = pltpu.SemaphoreType.DMA
    loss, grad = pl.pallas_call(
        functools.partial(step_kernel, R, C),
        out_shape=(
            jax.ShapeDtypeStruct((nodes,), F32),
            jax.ShapeDtypeStruct((width, width), F32),
        ),
        in_specs=[held] * 7,
        out_specs=(vmem, vmem),
        scratch_shapes=[
            pltpu.VMEM(weight.shape, BF16),
            pltpu.VMEM(tiles.shape, BF16),
            pltpu.SMEM(tile_pos.shape, jnp.int32),
            pltpu.SMEM(edge_keep.shape, jnp.int32),
            pltpu.VMEM(feature_keep.shape, jnp.int32),
            pltpu.VMEM(negatives.shape, jnp.int32),
            pltpu.VMEM((negatives.shape[1], negatives.shape[1]), BF16),
            pltpu.VMEM(negatives.shape, jnp.int32),
            pltpu.VMEM((nodes, group), F32),
            [pltpu.VMEM((C, nodes, 128), BF16)] * halves,
            pltpu.VMEM((halves, slots, 128, 128), F32),
            pltpu.VMEM((halves, R, 2, nodes, 128), BF16),
            pltpu.VMEM((halves, R, 2, nodes, 128), BF16),
            pltpu.VMEM((R, 2, nodes, width), BF16),
            pltpu.VMEM((R, 2, nodes, width), F32),
            pltpu.VMEM((R, 2, nodes, width), BF16),
            pltpu.VMEM((R, 2, nodes, 1), F32),
            pltpu.VMEM((R, 2, nodes, 128), F32),
            pltpu.VMEM((R, width, 2 * nodes), BF16),
            pltpu.VMEM((R, 2 * nodes, 2 * width), BF16),
            pltpu.VMEM((width // 2, width), F32),
            pltpu.VMEM((width // 2, width), F32),
            pltpu.VMEM((peers * piece_rows, width), F32),
            pltpu.VMEM((peers, piece_rows, width), F32),
            pltpu.VMEM((2, peers * piece_rows, width), F32),
            sem((halves, chips)), sem((halves, chips)), sem((halves, chips)), sem((halves, chips)),
            sem((halves, R)), sem((halves, R)), sem((halves, R)), sem((halves, R)),
            sem, sem, sem((peers,)), sem((peers,)),
            sem((peers,)), sem((peers,)), sem, sem, sem((6 + halves,)),
        ],
        compiler_params=pltpu.CompilerParams(
            collective_id=0, has_side_effects=True, vmem_limit_bytes=60 << 20
        ),
    )(features, weight, tiles, tile_pos, edge_keep, feature_keep, negatives)
    return pl.pallas_call(
        hand_over,
        out_shape=(
            jax.ShapeDtypeStruct((nodes,), F32),
            jax.ShapeDtypeStruct((width, width), F32),
        ),
        in_specs=[held] * 2,
        out_specs=(held, held),
        scratch_shapes=[pltpu.VMEM((nodes,), F32), pltpu.VMEM((width, width), F32), sem((5,)), sem((5,))],
        compiler_params=pltpu.CompilerParams(vmem_limit_bytes=60 << 20),
    )(loss, grad)


def solution(mesh):
    in_specs = (
        P(("row", "col"), None),
        P(),
        P(("row", "col"), None, None),
        P(("row", "col")),
        P(None, ("row", "col")),
        P(),
        P(("row", "col"), None),
    )
    out_specs = (P(("row", "col")), P())
    return jax.shard_map(shards, mesh=mesh, in_specs=in_specs, out_specs=out_specs, check_vma=False)
```

```python
import functools

import jax
import jax.numpy as jnp
from jax import lax
from jax.experimental import pallas as pl
from jax.experimental.pallas import tpu as pltpu
from jax.sharding import PartitionSpec as P

tau = 0.5
eps = 1e-06
F32 = jnp.float32
BF16 = jnp.bfloat16
MESH = pl.DeviceIdType.MESH


def loop(start, stop, body):
    if stop - start <= 16:
        for i in range(start, stop):
            body(i)
    else:
        def step(i, carry):
            body(i)
            return carry
        lax.fori_loop(start, stop, step, 0)


def spread_matrix(ref):
    n = ref.shape[0]
    stride = n // 128
    row = lax.broadcasted_iota(jnp.int32, (128, 128), 0)
    lane = lax.broadcasted_iota(jnp.int32, (128, 128), 1)
    for k in range(n // 128):
        here = lane == row // stride + k * (128 // stride)
        for s in range(stride):
            hit = jnp.logical_and(here, row % stride == s)
            ref[k * 128 : (k + 1) * 128, s * 128 : (s + 1) * 128] = jnp.where(hit, 1.0, 0.0).astype(BF16)


def spread(neg, matrix, out):
    low = (neg[...] & 255).astype(F32).astype(BF16)
    high = (neg[...] >> 8).astype(F32).astype(BF16)
    nodes = neg.shape[0]
    both = jnp.dot(jnp.concatenate([low, high], axis=0), matrix[...], preferred_element_type=F32)
    out[...] = (both[:nodes] + 256.0 * both[nodes:]).astype(jnp.int32)


def count_rows(i, tall, spread_ref, cnt):
    stride = spread_ref.shape[1] // 128
    blocks = cnt.shape[1] // 128
    per = 4 if blocks % 4 == 0 else 1
    rows = pl.ds(pl.multiple_of(i * tall, 8), tall)
    lane = lax.broadcasted_iota(jnp.int32, (tall, 128), 1)

    def take(part, index):
        return jnp.take_along_axis(part, index, axis=1, mode="promise_in_bounds")

    def block_step(g, before):
        starts = [pl.multiple_of((g * per + j) * 128, 128) for j in range(per)]
        targets = [lane + at for at in starts]
        last = spread_ref[rows, (stride - 1) * 128 : stride * 128]
        lows = [jnp.zeros((tall, 128), jnp.int32)] * per
        for step in (64, 32, 16, 8, 4, 2, 1):
            seen = [take(last, low + (step - 1)) for low in lows]
            lows = [jnp.where(x <= t, low + step, low) for x, t, low in zip(seen, targets, lows)]
        ranks = [low * stride for low in lows]
        for s in range(stride):
            part = spread_ref[rows, s * 128 : (s + 1) * 128]
            seen = [take(part, low) for low in lows]
            ranks = [jnp.where(x <= t, k + 1, k) for x, t, k in zip(seen, targets, ranks)]
        for at, now in zip(starts, ranks):
            rolled = pltpu.roll(now, 1, 1)
            cnt[rows, pl.ds(at, 128)] = (now - jnp.where(lane == 0, before, rolled)).astype(F32)
            before = rolled
        return before

    first = jnp.zeros((tall, 128), jnp.int32)
    if blocks == per:
        block_step(0, first)
    else:
        lax.fori_loop(0, blocks // per, block_step, first)


def step_kernel(
    R, C,
    feat, weight_in, tiles_in, pos_in, keep_in, fkeep_in, neg_in,
    loss_out, grad_out,
    weight, tiles, pos_ref, keep_ref, fkeep, neg, matrix, spread_ref, cnt,
    xg, prod, pbuf, rbuf, gbuf, embf, embb, rinv, eb, turned, dzb, wbuf, wsib, whalf, wr, obuf,
    f_send, f_recv, s_send, s_recv, p_send, p_recv, g_send, g_recv,
    a_send, a_recv, b_send, b_recv, c_send, c_recv, d_send, d_recv, l_sem,
):
    nodes, width = feat.shape
    halves = width // 128
    slots = tiles.shape[0]
    chips = C // 2
    peers = R * chips
    piece_rows = wr.shape[1]
    me_r = lax.axis_index("row")
    me_c = lax.axis_index("col")
    chip = me_c // 2
    core = me_c % 2
    sib = chip * 2 + (1 - core)

    paired = R <= 8 and R & (R - 1) == 0

    def partner(o):
        to = me_r
        for bit in range(3):
            if o >> bit & 1:
                to = to + (1 - 2 * (me_r // 2**bit % 2)) * 2**bit
        return to

    def at_row(o):
        return partner(o) if paired else lax.rem(me_r + o, R)

    def from_row(o):
        return partner(o) if paired else lax.rem(me_r + R - o, R)

    index = me_r * chips + chip

    def at_peer(o):
        to = lax.rem(index + o, peers)
        return to // chips, lax.rem(to, chips) * 2 + core

    def copy(src, dst, send, recv, r, c):
        return pltpu.make_async_remote_copy(
            src_ref=src, dst_ref=dst, send_sem=send, recv_sem=recv,
            device_id=(r, c), device_id_type=MESH,
        )

    loads = [
        pltpu.make_async_copy(neg_in, neg, l_sem.at[0]),
        pltpu.make_async_copy(tiles_in, tiles, l_sem.at[1]),
        pltpu.make_async_copy(weight_in, weight, l_sem.at[2]),
    ]
    for h in range(halves):
        loads.append(pltpu.make_async_copy(feat.at[:, h * 128 : (h + 1) * 128], xg[h].at[me_c], l_sem.at[3 + h]))
    loads.append(pltpu.make_async_copy(pos_in, pos_ref, l_sem.at[3 + halves]))
    loads.append(pltpu.make_async_copy(keep_in, keep_ref, l_sem.at[4 + halves]))
    loads.append(pltpu.make_async_copy(fkeep_in, fkeep, l_sem.at[5 + halves]))
    for load in loads:
        load.start()

    barrier = pltpu.get_barrier_semaphore()
    loop(1, peers, lambda o: pl.semaphore_signal(barrier, inc=1, device_id=at_peer(o), device_id_type=MESH))
    pl.semaphore_signal(barrier, inc=1, device_id=(me_r, sib), device_id_type=MESH)
    spread_matrix(matrix)
    pl.semaphore_wait(barrier, peers)

    def far(h, o):
        to = lax.rem(chip + o, chips) * 2 + core
        return copy(feat.at[:, h * 128 : (h + 1) * 128], xg[h].at[me_c], f_send.at[h, o], f_recv.at[h, o], me_r, to)

    def near(h, o):
        if isinstance(o, int) and o == 0:
            return copy(feat.at[:, h * 128 : (h + 1) * 128], xg[h].at[me_c], s_send.at[h, 0], s_recv.at[h, 0], me_r, sib)
        slot = lax.rem(chip + chips - o, chips) * 2 + core
        return copy(xg[h].at[slot], xg[h].at[slot], s_send.at[h, o], s_recv.at[h, o], me_r, sib)

    for h in range(halves):
        loop(1, chips, lambda o: far(h, o).start())
        near(h, 0).start()
    loads[0].wait()
    spread(neg, matrix, spread_ref)
    tall = 32
    turns = nodes // tall
    count_rows(0, tall, spread_ref, cnt)

    for load in loads[3 + halves :]:
        load.wait()
    where = [jnp.maximum(pos_ref[k], 0) for k in range(slots)]
    trow = [w // C for w in where]
    live = [[keep_ref[v, k] * (pos_ref[k] >= 0).astype(jnp.int32) for k in range(slots)] for v in range(2)]

    def part_copy(h, o):
        return copy(pbuf.at[h, o], rbuf.at[h, o], p_send.at[h, o], p_recv.at[h, o], at_row(o), me_c)

    def part(h, o):
        t = at_row(o)
        here = [trow[k] == t for k in range(slots)]
        for v in range(2):
            total = None
            for k in range(slots):
                term = prod[h, k] * jnp.where(here[k], live[v][k], 0).astype(F32)
                total = term if total is None else total + term
            pbuf[h, o, v] = total.astype(BF16)

    for h in range(halves):
        def pass_on(o):
            far(h, o).wait_recv()
            near(h, o).start()

        loop(1, chips, pass_on)
        near(h, 0).wait_recv()
        loop(1, chips, lambda o: near(h, o).wait_recv())
        loads[3 + h].wait()
        if h == 0:
            loads[1].wait()
        for k in range(slots):
            prod[h, k] = jnp.dot(tiles[k], xg[h][lax.rem(where[k], C)], preferred_element_type=F32)

        def part_send(o):
            part(h, o)
            part_copy(h, o).start()

        loop(1, R, lambda o: part_send(R - o))

    count_rows(1, tall, spread_ref, cnt)

    def agg_copy(h, o):
        ref = gbuf.at[me_r, :, :, h * 128 : (h + 1) * 128]
        return copy(ref, ref, g_send.at[h, o], g_recv.at[h, o], at_row(o), me_c)

    for h in range(halves):
        part(h, 0)
        loop(1, R, lambda o: part_copy(h, o).wait_recv())
        for v in range(2):
            total = pbuf[h, 0, v].astype(F32)
            if R <= 8:
                for o in range(1, R):
                    total = total + rbuf[h, o, v].astype(F32)
            else:
                total = lax.fori_loop(1, R, lambda o, acc: acc + rbuf[h, o, v].astype(F32), total)
            total = total * fkeep[v : v + 1, h * 128 : (h + 1) * 128].astype(F32)
            gbuf[me_r, v, :, h * 128 : (h + 1) * 128] = total.astype(BF16)
        loop(1, R, lambda o: agg_copy(h, o).start())
    for i in range(2, turns):
        count_rows(i, tall, spread_ref, cnt)
    loads[2].wait()

    def embed(r):
        stacked = gbuf[r].reshape(2 * nodes, width)
        z = jnp.dot(stacked, weight[...], preferred_element_type=F32)
        scale = lax.rsqrt(jnp.sum(z * z, -1, keepdims=True) + eps)
        emb = z * scale
        rinv[r] = scale.reshape(2, nodes, 1)
        embf[r] = emb.reshape(2, nodes, width)
        embb[r] = emb.astype(BF16).reshape(2, nodes, width)
        turned[r] = stacked.T

    embed(me_r)
    h1 = embb[me_r, 0]
    h2 = embb[me_r, 1]
    h1f = h1.astype(F32)
    h2f = h2.astype(F32)
    pos = jnp.sum(h1f * h2f, -1, keepdims=True) / tau
    NT = (((1,), (1,)), ((), ()))
    TN = (((0,), (0,)), ((), ()))

    def scores(r):
        cols = pl.ds(pl.multiple_of(r * 128, 128), 128)
        counts = cnt[:, cols]
        s12 = lax.dot_general(h1, embb[r, 1], NT, preferred_element_type=F32) / tau
        s21 = lax.dot_general(h2, embb[r, 0], NT, preferred_element_type=F32) / tau
        eb[r, 0] = counts * jnp.exp(s12)
        eb[r, 1] = counts * jnp.exp(s21)

    scores(me_r)

    def arrived(o):
        r = from_row(o)
        for h in range(halves):
            agg_copy(h, o).wait_recv()
        embed(r)
        scores(r)

    loop(1, R, arrived)

    def row_sum(v):
        if R <= 8:
            total = eb[0, v]
            for r in range(1, R):
                total = total + eb[r, v]
        else:
            total = lax.fori_loop(1, R, lambda r, acc: acc + eb[r, v], eb[0, v])
        return jnp.sum(total, 1, keepdims=True)

    epos = jnp.exp(pos)
    tot1 = epos + row_sum(0)
    tot2 = epos + row_sum(1)
    loss = 0.5 * (jnp.log(tot1) - pos + (jnp.log(tot2) - pos))
    both = epos / tot1 + epos / tot2 - 2.0
    coef = 1.0 / (2.0 * tau * float(R * C * nodes) ** 0.5)

    def dz_term(r, d_one, d_two):
        for v, d in enumerate((d_one, d_two)):
            emb = embf[r, v]
            dz = (d - emb * jnp.sum(emb * d, -1, keepdims=True)) * rinv[r, v]
            high = dz.astype(BF16)
            dzb[r, v * nodes : (v + 1) * nodes, :width] = high
            dzb[r, v * nodes : (v + 1) * nodes, width:] = (dz - high.astype(F32)).astype(BF16)

    def weights(r):
        q1 = (eb[r, 0] / tot1).astype(BF16)
        q2 = (eb[r, 1] / tot2).astype(BF16)
        fore1 = jnp.dot(q1, embb[r, 1], preferred_element_type=F32)
        fore2 = jnp.dot(q2, embb[r, 0], preferred_element_type=F32)
        back1 = lax.dot_general(q2, h2, TN, preferred_element_type=F32)
        back2 = lax.dot_general(q1, h1, TN, preferred_element_type=F32)
        return fore1, fore2, back1, back2

    acc1, acc2, own1, own2 = weights(me_r)

    def other(o, carry):
        r = from_row(o)
        fore1, fore2, back1, back2 = weights(r)
        dz_term(r, coef * back1, coef * back2)
        return carry[0] + fore1, carry[1] + fore2

    if R <= 8:
        for o in range(1, R):
            acc1, acc2 = other(o, (acc1, acc2))
    else:
        acc1, acc2 = lax.fori_loop(1, R, other, (acc1, acc2))
    dz_term(
        me_r, coef * (both * h2f + acc1 + own1), coef * (both * h1f + acc2 + own2)
    )

    half = width // 2

    def grad_half(side):
        rows = pl.ds(pl.multiple_of(side * half, 16), half)

        def term(r):
            return jnp.dot(turned[r, rows, :], dzb[r], preferred_element_type=F32)

        if R <= 8:
            terms = term(0)
            for r in range(1, R):
                terms = terms + term(r)
        else:
            terms = lax.fori_loop(1, R, lambda r, acc: acc + term(r), term(0))
        return terms[:, :width] + terms[:, width:]

    wbuf[...] = grad_half(1 - core)
    a_copy = copy(wbuf, wsib, a_send, a_recv, me_r, sib)
    a_copy.start()
    own = grad_half(core)
    if whalf.shape[0] > half:
        whalf[...] = jnp.zeros_like(whalf)
    a_copy.wait_recv()
    whalf[0:half, :] = own + wsib[...]

    def b_copy(o):
        to = lax.rem(index + o, peers)
        rows = pl.ds(pl.multiple_of(to * piece_rows, 8), piece_rows)
        r, c = at_peer(o)
        return copy(whalf.at[rows, :], wr.at[o], b_send.at[o], b_recv.at[o], r, c)

    loop(1, peers, lambda o: b_copy(o).start())
    loss_out[...] = jnp.broadcast_to(loss, (nodes, 128)).T[0]
    my_rows = pl.ds(pl.multiple_of(index * piece_rows, 8), piece_rows)
    piece = whalf[my_rows, :]
    loop(1, peers, lambda o: b_copy(o).wait_recv())
    if peers <= 32:
        for o in range(1, peers):
            piece = piece + wr[o]
    else:
        piece = lax.fori_loop(1, peers, lambda o, acc: acc + wr[o], piece)
    obuf[core, my_rows, :] = piece

    def c_copy(o):
        r, c = at_peer(o)
        ref = obuf.at[core, my_rows, :]
        return copy(ref, ref, c_send.at[o], c_recv.at[o], r, c)

    loop(1, peers, lambda o: c_copy(o).start())
    loop(1, peers, lambda o: c_copy(o).wait_recv())
    mine_done = obuf.at[core, pl.ds(0, half), :]
    d_copy = copy(mine_done, mine_done, d_send, d_recv, me_r, sib)
    d_copy.start()
    my_half = pl.ds(pl.multiple_of(core * half, 8), half)
    grad_out[my_half, :] = obuf[core, 0:half, :]
    d_copy.wait_recv()
    its_half = pl.ds(pl.multiple_of((1 - core) * half, 8), half)
    grad_out[its_half, :] = obuf[1 - core, 0:half, :]

    for h in range(halves):
        loop(1, chips, lambda o: far(h, o).wait_send())
        near(h, 0).wait_send()
        loop(1, chips, lambda o: near(h, o).wait_send())
        loop(1, R, lambda o: part_copy(h, o).wait_send())
        loop(1, R, lambda o: agg_copy(h, o).wait_send())
    a_copy.wait_send()
    loop(1, peers, lambda o: b_copy(o).wait_send())
    loop(1, peers, lambda o: c_copy(o).wait_send())
    d_copy.wait_send()


def hand_over(loss, grad, loss_out, grad_out, loss_buf, grad_buf, in_sems, out_sems):
    chunks = out_sems.shape[0] - 1
    rows = grad.shape[0] // chunks
    ins = [pltpu.make_async_copy(loss, loss_buf, in_sems.at[chunks])]
    outs = [pltpu.make_async_copy(loss_buf, loss_out, out_sems.at[chunks])]
    for i in range(chunks):
        part = pl.ds(i * rows, rows)
        ins.append(pltpu.make_async_copy(grad.at[part, :], grad_buf.at[part, :], in_sems.at[i]))
        outs.append(pltpu.make_async_copy(grad_buf.at[part, :], grad_out.at[part, :], out_sems.at[i]))
    for move in ins:
        move.start()
    for move, then in zip(ins, outs):
        move.wait()
        then.start()
    for move in outs:
        move.wait()


def up(n, d, unit):
    return -(-(-(-n // d)) // unit) * unit


def shards(features, weight, tiles, tile_pos, edge_keep, feature_keep, negatives):
    nodes, width = features.shape
    halves = width // 128
    slots = tiles.shape[0]
    R = lax.axis_size("row")
    C = lax.axis_size("col")
    group = R * nodes
    chips = C // 2
    peers = R * chips
    piece_rows = up(width // 2, peers, 8)
    vmem = pl.BlockSpec(memory_space=pltpu.VMEM)
    held = pl.BlockSpec(memory_space=pl.ANY)
    sem = pltpu.SemaphoreType.DMA
    loss, grad = pl.pallas_call(
        functools.partial(step_kernel, R, C),
        out_shape=(
            jax.ShapeDtypeStruct((nodes,), F32),
            jax.ShapeDtypeStruct((width, width), F32),
        ),
        in_specs=[held] * 7,
        out_specs=(vmem, vmem),
        scratch_shapes=[
            pltpu.VMEM(weight.shape, BF16),
            pltpu.VMEM(tiles.shape, BF16),
            pltpu.SMEM(tile_pos.shape, jnp.int32),
            pltpu.SMEM(edge_keep.shape, jnp.int32),
            pltpu.VMEM(feature_keep.shape, jnp.int32),
            pltpu.VMEM(negatives.shape, jnp.int32),
            pltpu.VMEM((negatives.shape[1], negatives.shape[1]), BF16),
            pltpu.VMEM(negatives.shape, jnp.int32),
            pltpu.VMEM((nodes, group), F32),
            [pltpu.VMEM((C, nodes, 128), BF16)] * halves,
            pltpu.VMEM((halves, slots, 128, 128), F32),
            pltpu.VMEM((halves, R, 2, nodes, 128), BF16),
            pltpu.VMEM((halves, R, 2, nodes, 128), BF16),
            pltpu.VMEM((R, 2, nodes, width), BF16),
            pltpu.VMEM((R, 2, nodes, width), F32),
            pltpu.VMEM((R, 2, nodes, width), BF16),
            pltpu.VMEM((R, 2, nodes, 1), F32),
            pltpu.VMEM((R, 2, nodes, 128), F32),
            pltpu.VMEM((R, width, 2 * nodes), BF16),
            pltpu.VMEM((R, 2 * nodes, 2 * width), BF16),
            pltpu.VMEM((width // 2, width), F32),
            pltpu.VMEM((width // 2, width), F32),
            pltpu.VMEM((peers * piece_rows, width), F32),
            pltpu.VMEM((peers, piece_rows, width), F32),
            pltpu.VMEM((2, peers * piece_rows, width), F32),
            sem((halves, chips)), sem((halves, chips)), sem((halves, chips)), sem((halves, chips)),
            sem((halves, R)), sem((halves, R)), sem((halves, R)), sem((halves, R)),
            sem, sem, sem((peers,)), sem((peers,)),
            sem((peers,)), sem((peers,)), sem, sem, sem((6 + halves,)),
        ],
        compiler_params=pltpu.CompilerParams(
            collective_id=0, has_side_effects=True, vmem_limit_bytes=60 << 20
        ),
    )(features, weight, tiles, tile_pos, edge_keep, feature_keep, negatives)
    return pl.pallas_call(
        hand_over,
        out_shape=(
            jax.ShapeDtypeStruct((nodes,), F32),
            jax.ShapeDtypeStruct((width, width), F32),
        ),
        in_specs=[held] * 2,
        out_specs=(held, held),
        scratch_shapes=[pltpu.VMEM((nodes,), F32), pltpu.VMEM((width, width), F32), sem((5,)), sem((5,))],
        compiler_params=pltpu.CompilerParams(vmem_limit_bytes=60 << 20),
    )(loss, grad)


def solution(mesh):
    in_specs = (
        P(("row", "col"), None),
        P(),
        P(("row", "col"), None, None),
        P(("row", "col")),
        P(None, ("row", "col")),
        P(),
        P(("row", "col"), None),
    )
    out_specs = (P(("row", "col")), P())
    return jax.shard_map(shards, mesh=mesh, in_specs=in_specs, out_specs=out_specs, check_vma=False)
```

```python
import functools

import jax
import jax.numpy as jnp
from jax import lax
from jax.experimental import pallas as pl
from jax.experimental.pallas import tpu as pltpu
from jax.sharding import PartitionSpec as P

tau = 0.5
eps = 1e-06
F32 = jnp.float32
BF16 = jnp.bfloat16
MESH = pl.DeviceIdType.MESH


def loop(start, stop, body):
    if stop - start <= 16:
        for i in range(start, stop):
            body(i)
    else:
        def step(i, carry):
            body(i)
            return carry
        lax.fori_loop(start, stop, step, 0)


def spread_matrix(ref):
    n = ref.shape[0]
    stride = n // 128
    row = lax.broadcasted_iota(jnp.int32, (128, 128), 0)
    lane = lax.broadcasted_iota(jnp.int32, (128, 128), 1)
    for k in range(n // 128):
        here = lane == row // stride + k * (128 // stride)
        for s in range(stride):
            hit = jnp.logical_and(here, row % stride == s)
            ref[k * 128 : (k + 1) * 128, s * 128 : (s + 1) * 128] = jnp.where(hit, 1.0, 0.0).astype(BF16)


def spread(neg, matrix, out):
    low = (neg[...] & 255).astype(F32).astype(BF16)
    high = (neg[...] >> 8).astype(F32).astype(BF16)
    nodes = neg.shape[0]
    both = jnp.dot(jnp.concatenate([low, high], axis=0), matrix[...], preferred_element_type=F32)
    out[...] = (both[:nodes] + 256.0 * both[nodes:]).astype(jnp.int32)


def count_rows(i, tall, spread_ref, cnt):
    stride = spread_ref.shape[1] // 128
    blocks = cnt.shape[1] // 128
    per = 4 if blocks % 4 == 0 else 1
    rows = pl.ds(pl.multiple_of(i * tall, 8), tall)
    lane = lax.broadcasted_iota(jnp.int32, (tall, 128), 1)

    def take(part, index):
        return jnp.take_along_axis(part, index, axis=1, mode="promise_in_bounds")

    def block_step(g, before):
        starts = [pl.multiple_of((g * per + j) * 128, 128) for j in range(per)]
        targets = [lane + at for at in starts]
        last = spread_ref[rows, (stride - 1) * 128 : stride * 128]
        lows = [jnp.zeros((tall, 128), jnp.int32)] * per
        for step in (64, 32, 16, 8, 4, 2, 1):
            seen = [take(last, low + (step - 1)) for low in lows]
            lows = [jnp.where(x <= t, low + step, low) for x, t, low in zip(seen, targets, lows)]
        ranks = [low * stride for low in lows]
        for s in range(stride):
            part = spread_ref[rows, s * 128 : (s + 1) * 128]
            seen = [take(part, low) for low in lows]
            ranks = [jnp.where(x <= t, k + 1, k) for x, t, k in zip(seen, targets, ranks)]
        for at, now in zip(starts, ranks):
            rolled = pltpu.roll(now, 1, 1)
            cnt[rows, pl.ds(at, 128)] = (now - jnp.where(lane == 0, before, rolled)).astype(F32)
            before = rolled
        return before

    first = jnp.zeros((tall, 128), jnp.int32)
    if blocks == per:
        block_step(0, first)
    else:
        lax.fori_loop(0, blocks // per, block_step, first)


def step_kernel(
    R, C,
    feat, weight_in, tiles_in, pos_in, keep_in, fkeep_in, neg_in,
    loss_out, grad_out,
    weight, tiles, pos_ref, keep_ref, fkeep, neg, matrix, spread_ref, cnt,
    xg, prod, pbuf, rbuf, gbuf, embf, embb, rinv, eb, turned, dzb, wbuf, wsib, whalf, wr, obuf,
    f_send, f_recv, s_send, s_recv, p_send, p_recv, g_send, g_recv,
    a_send, a_recv, b_send, b_recv, c_send, c_recv, d_send, d_recv, l_sem,
):
    nodes, width = feat.shape
    halves = width // 128
    slots = tiles.shape[0]
    chips = C // 2
    peers = R * chips
    piece_rows = wr.shape[1]
    me_r = lax.axis_index("row")
    me_c = lax.axis_index("col")
    chip = me_c // 2
    core = me_c % 2
    sib = chip * 2 + (1 - core)

    paired = R <= 8 and R & (R - 1) == 0

    def partner(o):
        to = me_r
        for bit in range(3):
            if o >> bit & 1:
                to = to + (1 - 2 * (me_r // 2**bit % 2)) * 2**bit
        return to

    def at_row(o):
        return partner(o) if paired else lax.rem(me_r + o, R)

    def from_row(o):
        return partner(o) if paired else lax.rem(me_r + R - o, R)

    index = me_r * chips + chip

    def at_peer(o):
        to = lax.rem(index + o, peers)
        return to // chips, lax.rem(to, chips) * 2 + core

    def copy(src, dst, send, recv, r, c):
        return pltpu.make_async_remote_copy(
            src_ref=src, dst_ref=dst, send_sem=send, recv_sem=recv,
            device_id=(r, c), device_id_type=MESH,
        )

    loads = [
        pltpu.make_async_copy(neg_in, neg, l_sem.at[0]),
        pltpu.make_async_copy(tiles_in, tiles, l_sem.at[1]),
        pltpu.make_async_copy(weight_in, weight, l_sem.at[2]),
    ]
    for h in range(halves):
        loads.append(pltpu.make_async_copy(feat.at[:, h * 128 : (h + 1) * 128], xg[h].at[me_c], l_sem.at[3 + h]))
    loads.append(pltpu.make_async_copy(pos_in, pos_ref, l_sem.at[3 + halves]))
    loads.append(pltpu.make_async_copy(keep_in, keep_ref, l_sem.at[4 + halves]))
    loads.append(pltpu.make_async_copy(fkeep_in, fkeep, l_sem.at[5 + halves]))
    for load in loads:
        load.start()

    barrier = pltpu.get_barrier_semaphore()
    loop(1, peers, lambda o: pl.semaphore_signal(barrier, inc=1, device_id=at_peer(o), device_id_type=MESH))
    pl.semaphore_signal(barrier, inc=1, device_id=(me_r, sib), device_id_type=MESH)
    spread_matrix(matrix)
    pl.semaphore_wait(barrier, peers)

    def far(h, o):
        to = lax.rem(chip + o, chips) * 2 + core
        return copy(feat.at[:, h * 128 : (h + 1) * 128], xg[h].at[me_c], f_send.at[h, o], f_recv.at[h, o], me_r, to)

    def near(h, o):
        if isinstance(o, int) and o == 0:
            return copy(feat.at[:, h * 128 : (h + 1) * 128], xg[h].at[me_c], s_send.at[h, 0], s_recv.at[h, 0], me_r, sib)
        slot = lax.rem(chip + chips - o, chips) * 2 + core
        return copy(xg[h].at[slot], xg[h].at[slot], s_send.at[h, o], s_recv.at[h, o], me_r, sib)

    for h in range(halves):
        loop(1, chips, lambda o: far(h, o).start())
        near(h, 0).start()
    loads[0].wait()
    spread(neg, matrix, spread_ref)
    tall = 32
    turns = nodes // tall

    for load in loads[3 + halves :]:
        load.wait()
    where = [jnp.maximum(pos_ref[k], 0) for k in range(slots)]
    trow = [w // C for w in where]
    live = [[keep_ref[v, k] * (pos_ref[k] >= 0).astype(jnp.int32) for k in range(slots)] for v in range(2)]

    def part_copy(h, o):
        return copy(pbuf.at[h, o], rbuf.at[h, o], p_send.at[h, o], p_recv.at[h, o], at_row(o), me_c)

    def part(h, o):
        t = at_row(o)
        here = [trow[k] == t for k in range(slots)]
        for v in range(2):
            total = None
            for k in range(slots):
                term = prod[h, k] * jnp.where(here[k], live[v][k], 0).astype(F32)
                total = term if total is None else total + term
            pbuf[h, o, v] = total.astype(BF16)

    for h in range(halves):
        def pass_on(o):
            far(h, o).wait_recv()
            near(h, o).start()

        loop(1, chips, pass_on)
        if h == 0:
            count_rows(0, tall, spread_ref, cnt)
        near(h, 0).wait_recv()
        loop(1, chips, lambda o: near(h, o).wait_recv())
        loads[3 + h].wait()
        if h == 0:
            loads[1].wait()
        for k in range(slots):
            prod[h, k] = jnp.dot(tiles[k], xg[h][lax.rem(where[k], C)], preferred_element_type=F32)

        def part_send(o):
            part(h, o)
            part_copy(h, o).start()

        loop(1, R, lambda o: part_send(R - o))

    count_rows(1, tall, spread_ref, cnt)

    def agg_copy(h, o):
        ref = gbuf.at[me_r, :, :, h * 128 : (h + 1) * 128]
        return copy(ref, ref, g_send.at[h, o], g_recv.at[h, o], at_row(o), me_c)

    for h in range(halves):
        part(h, 0)
        loop(1, R, lambda o: part_copy(h, o).wait_recv())
        for v in range(2):
            total = pbuf[h, 0, v].astype(F32)
            if R <= 8:
                for o in range(1, R):
                    total = total + rbuf[h, o, v].astype(F32)
            else:
                total = lax.fori_loop(1, R, lambda o, acc: acc + rbuf[h, o, v].astype(F32), total)
            total = total * fkeep[v : v + 1, h * 128 : (h + 1) * 128].astype(F32)
            gbuf[me_r, v, :, h * 128 : (h + 1) * 128] = total.astype(BF16)
        loop(1, R, lambda o: agg_copy(h, o).start())
    for i in range(2, turns):
        count_rows(i, tall, spread_ref, cnt)
    loads[2].wait()

    def embed(r):
        stacked = gbuf[r].reshape(2 * nodes, width)
        z = jnp.dot(stacked, weight[...], preferred_element_type=F32)
        scale = lax.rsqrt(jnp.sum(z * z, -1, keepdims=True) + eps)
        emb = z * scale
        rinv[r] = scale.reshape(2, nodes, 1)
        embf[r] = emb.reshape(2, nodes, width)
        embb[r] = emb.astype(BF16).reshape(2, nodes, width)
        turned[r] = stacked.T

    embed(me_r)
    h1 = embb[me_r, 0]
    h2 = embb[me_r, 1]
    h1f = h1.astype(F32)
    h2f = h2.astype(F32)
    pos = jnp.sum(h1f * h2f, -1, keepdims=True) / tau
    NT = (((1,), (1,)), ((), ()))
    TN = (((0,), (0,)), ((), ()))

    def scores(r):
        cols = pl.ds(pl.multiple_of(r * 128, 128), 128)
        counts = cnt[:, cols]
        s12 = lax.dot_general(h1, embb[r, 1], NT, preferred_element_type=F32) / tau
        s21 = lax.dot_general(h2, embb[r, 0], NT, preferred_element_type=F32) / tau
        eb[r, 0] = counts * jnp.exp(s12)
        eb[r, 1] = counts * jnp.exp(s21)

    scores(me_r)

    def arrived(o):
        r = from_row(o)
        for h in range(halves):
            agg_copy(h, o).wait_recv()
        embed(r)
        scores(r)

    loop(1, R, arrived)

    def row_sum(v):
        if R <= 8:
            total = eb[0, v]
            for r in range(1, R):
                total = total + eb[r, v]
        else:
            total = lax.fori_loop(1, R, lambda r, acc: acc + eb[r, v], eb[0, v])
        return jnp.sum(total, 1, keepdims=True)

    epos = jnp.exp(pos)
    tot1 = epos + row_sum(0)
    tot2 = epos + row_sum(1)
    loss = 0.5 * (jnp.log(tot1) - pos + (jnp.log(tot2) - pos))
    both = epos / tot1 + epos / tot2 - 2.0
    coef = 1.0 / (2.0 * tau * float(R * C * nodes) ** 0.5)

    def dz_term(r, d_one, d_two):
        for v, d in enumerate((d_one, d_two)):
            emb = embf[r, v]
            dz = (d - emb * jnp.sum(emb * d, -1, keepdims=True)) * rinv[r, v]
            high = dz.astype(BF16)
            dzb[r, v * nodes : (v + 1) * nodes, :width] = high
            dzb[r, v * nodes : (v + 1) * nodes, width:] = (dz - high.astype(F32)).astype(BF16)

    def weights(r):
        q1 = (eb[r, 0] / tot1).astype(BF16)
        q2 = (eb[r, 1] / tot2).astype(BF16)
        fore1 = jnp.dot(q1, embb[r, 1], preferred_element_type=F32)
        fore2 = jnp.dot(q2, embb[r, 0], preferred_element_type=F32)
        back1 = lax.dot_general(q2, h2, TN, preferred_element_type=F32)
        back2 = lax.dot_general(q1, h1, TN, preferred_element_type=F32)
        return fore1, fore2, back1, back2

    acc1, acc2, own1, own2 = weights(me_r)

    def other(o, carry):
        r = from_row(o)
        fore1, fore2, back1, back2 = weights(r)
        dz_term(r, coef * back1, coef * back2)
        return carry[0] + fore1, carry[1] + fore2

    if R <= 8:
        for o in range(1, R):
            acc1, acc2 = other(o, (acc1, acc2))
    else:
        acc1, acc2 = lax.fori_loop(1, R, other, (acc1, acc2))
    dz_term(
        me_r, coef * (both * h2f + acc1 + own1), coef * (both * h1f + acc2 + own2)
    )

    half = width // 2

    def grad_half(side):
        rows = pl.ds(pl.multiple_of(side * half, 16), half)

        def term(r):
            return jnp.dot(turned[r, rows, :], dzb[r], preferred_element_type=F32)

        if R <= 8:
            terms = term(0)
            for r in range(1, R):
                terms = terms + term(r)
        else:
            terms = lax.fori_loop(1, R, lambda r, acc: acc + term(r), term(0))
        return terms[:, :width] + terms[:, width:]

    wbuf[...] = grad_half(1 - core)
    a_copy = copy(wbuf, wsib, a_send, a_recv, me_r, sib)
    a_copy.start()
    own = grad_half(core)
    if whalf.shape[0] > half:
        whalf[...] = jnp.zeros_like(whalf)
    a_copy.wait_recv()
    whalf[0:half, :] = own + wsib[...]

    def b_copy(o):
        to = lax.rem(index + o, peers)
        rows = pl.ds(pl.multiple_of(to * piece_rows, 8), piece_rows)
        r, c = at_peer(o)
        return copy(whalf.at[rows, :], wr.at[o], b_send.at[o], b_recv.at[o], r, c)

    loop(1, peers, lambda o: b_copy(o).start())
    loss_out[...] = jnp.broadcast_to(loss, (nodes, 128)).T[0]
    my_rows = pl.ds(pl.multiple_of(index * piece_rows, 8), piece_rows)
    piece = whalf[my_rows, :]
    loop(1, peers, lambda o: b_copy(o).wait_recv())
    if peers <= 32:
        for o in range(1, peers):
            piece = piece + wr[o]
    else:
        piece = lax.fori_loop(1, peers, lambda o, acc: acc + wr[o], piece)
    obuf[core, my_rows, :] = piece

    def c_copy(o):
        r, c = at_peer(o)
        ref = obuf.at[core, my_rows, :]
        return copy(ref, ref, c_send.at[o], c_recv.at[o], r, c)

    loop(1, peers, lambda o: c_copy(o).start())
    loop(1, peers, lambda o: c_copy(o).wait_recv())
    mine_done = obuf.at[core, pl.ds(0, half), :]
    d_copy = copy(mine_done, mine_done, d_send, d_recv, me_r, sib)
    d_copy.start()
    my_half = pl.ds(pl.multiple_of(core * half, 8), half)
    grad_out[my_half, :] = obuf[core, 0:half, :]
    d_copy.wait_recv()
    its_half = pl.ds(pl.multiple_of((1 - core) * half, 8), half)
    grad_out[its_half, :] = obuf[1 - core, 0:half, :]

    for h in range(halves):
        loop(1, chips, lambda o: far(h, o).wait_send())
        near(h, 0).wait_send()
        loop(1, chips, lambda o: near(h, o).wait_send())
        loop(1, R, lambda o: part_copy(h, o).wait_send())
        loop(1, R, lambda o: agg_copy(h, o).wait_send())
    a_copy.wait_send()
    loop(1, peers, lambda o: b_copy(o).wait_send())
    loop(1, peers, lambda o: c_copy(o).wait_send())
    d_copy.wait_send()


def hand_over(loss, grad, loss_out, grad_out, loss_buf, grad_buf, in_sems, out_sems):
    chunks = out_sems.shape[0] - 1
    rows = grad.shape[0] // chunks
    ins = [pltpu.make_async_copy(loss, loss_buf, in_sems.at[chunks])]
    outs = [pltpu.make_async_copy(loss_buf, loss_out, out_sems.at[chunks])]
    for i in range(chunks):
        part = pl.ds(i * rows, rows)
        ins.append(pltpu.make_async_copy(grad.at[part, :], grad_buf.at[part, :], in_sems.at[i]))
        outs.append(pltpu.make_async_copy(grad_buf.at[part, :], grad_out.at[part, :], out_sems.at[i]))
    for move in ins:
        move.start()
    for move, then in zip(ins, outs):
        move.wait()
        then.start()
    for move in outs:
        move.wait()


def up(n, d, unit):
    return -(-(-(-n // d)) // unit) * unit


def shards(features, weight, tiles, tile_pos, edge_keep, feature_keep, negatives):
    nodes, width = features.shape
    halves = width // 128
    slots = tiles.shape[0]
    R = lax.axis_size("row")
    C = lax.axis_size("col")
    group = R * nodes
    chips = C // 2
    peers = R * chips
    piece_rows = up(width // 2, peers, 8)
    vmem = pl.BlockSpec(memory_space=pltpu.VMEM)
    held = pl.BlockSpec(memory_space=pl.ANY)
    sem = pltpu.SemaphoreType.DMA
    loss, grad = pl.pallas_call(
        functools.partial(step_kernel, R, C),
        out_shape=(
            jax.ShapeDtypeStruct((nodes,), F32),
            jax.ShapeDtypeStruct((width, width), F32),
        ),
        in_specs=[held] * 7,
        out_specs=(vmem, vmem),
        scratch_shapes=[
            pltpu.VMEM(weight.shape, BF16),
            pltpu.VMEM(tiles.shape, BF16),
            pltpu.SMEM(tile_pos.shape, jnp.int32),
            pltpu.SMEM(edge_keep.shape, jnp.int32),
            pltpu.VMEM(feature_keep.shape, jnp.int32),
            pltpu.VMEM(negatives.shape, jnp.int32),
            pltpu.VMEM((negatives.shape[1], negatives.shape[1]), BF16),
            pltpu.VMEM(negatives.shape, jnp.int32),
            pltpu.VMEM((nodes, group), F32),
            [pltpu.VMEM((C, nodes, 128), BF16)] * halves,
            pltpu.VMEM((halves, slots, 128, 128), F32),
            pltpu.VMEM((halves, R, 2, nodes, 128), BF16),
            pltpu.VMEM((halves, R, 2, nodes, 128), BF16),
            pltpu.VMEM((R, 2, nodes, width), BF16),
            pltpu.VMEM((R, 2, nodes, width), F32),
            pltpu.VMEM((R, 2, nodes, width), BF16),
            pltpu.VMEM((R, 2, nodes, 1), F32),
            pltpu.VMEM((R, 2, nodes, 128), F32),
            pltpu.VMEM((R, width, 2 * nodes), BF16),
            pltpu.VMEM((R, 2 * nodes, 2 * width), BF16),
            pltpu.VMEM((width // 2, width), F32),
            pltpu.VMEM((width // 2, width), F32),
            pltpu.VMEM((peers * piece_rows, width), F32),
            pltpu.VMEM((peers, piece_rows, width), F32),
            pltpu.VMEM((2, peers * piece_rows, width), F32),
            sem((halves, chips)), sem((halves, chips)), sem((halves, chips)), sem((halves, chips)),
            sem((halves, R)), sem((halves, R)), sem((halves, R)), sem((halves, R)),
            sem, sem, sem((peers,)), sem((peers,)),
            sem((peers,)), sem((peers,)), sem, sem, sem((6 + halves,)),
        ],
        compiler_params=pltpu.CompilerParams(
            collective_id=0, has_side_effects=True, vmem_limit_bytes=60 << 20
        ),
    )(features, weight, tiles, tile_pos, edge_keep, feature_keep, negatives)
    return pl.pallas_call(
        hand_over,
        out_shape=(
            jax.ShapeDtypeStruct((nodes,), F32),
            jax.ShapeDtypeStruct((width, width), F32),
        ),
        in_specs=[held] * 2,
        out_specs=(held, held),
        scratch_shapes=[pltpu.VMEM((nodes,), F32), pltpu.VMEM((width, width), F32), sem((5,)), sem((5,))],
        compiler_params=pltpu.CompilerParams(vmem_limit_bytes=60 << 20),
    )(loss, grad)


def solution(mesh):
    in_specs = (
        P(("row", "col"), None),
        P(),
        P(("row", "col"), None, None),
        P(("row", "col")),
        P(None, ("row", "col")),
        P(),
        P(("row", "col"), None),
    )
    out_specs = (P(("row", "col")), P())
    return jax.shard_map(shards, mesh=mesh, in_specs=in_specs, out_specs=out_specs, check_vma=False)
```
